32 devices in a mesh: dp: 32 (over z, y, x, core).
Axes of the slice: x: 2, y: 2, z: 4, core: 2. Of those that a mesh axis runs over, the one named last changes fastest.
Arguments:
- tokens: bfloat16 [100864, 384], P('dp'), may hold values from -6 to 6
- attn_weights: bfloat16 [1536, 384], P('dp')
- expert_in: bfloat16 [3072, 1536], P('dp'), may hold values from -0.3125 to 0.3125
- expert_out: bfloat16 [12288, 384], P('dp'), may hold values from -0.625 to 0.625
- gain_one: float32 [384], replicated, may hold values from 0.5 to 1.5
- gain_two: float32 [384], replicated, may hold values from 0.5 to 1.5
- router: float32 [384, 8], replicated, may hold values from -0.21875 to 0.21875
- routes: int32 [100864, 2], P('dp'), may hold values from 0 to 7, as said below
- slots: int32 [100864, 2], P('dp'), may hold values from 0 to 788, as said below
- cotangent: bfloat16 [100864, 384], P('dp'), may hold values from -6 to 6
Outputs:
- output: bfloat16 [100864, 384], P('dp')
- grad_tokens: bfloat16 [100864, 384], P('dp')
- grad_attn_weights: float32 [1536, 384], P('dp')
- grad_expert_in: float32 [3072, 1536], P('dp')
- grad_expert_out: float32 [12288, 384], P('dp')
- grad_gain_one: float32 [384], replicated
- grad_gain_two: float32 [384], replicated
- grad_router: float32 [384, 8], replicated
The draws below stay inside these ranges and needn't reach their ends.
Inputs may be any that keep to these rules, and one draw needn't show every extreme that they name: `routes`: the two experts of a token differ. On each device's 3152 tokens, the first choices in token order and then the second choices take the free slots 0, 1, 2 ... of their expert in turn; a pair that finds its expert's 788 slots taken gets 788 and is dropped.
All inputs are finite; a program needn't handle non-finite values.
Results may differ from the reference program's by a relative error of at most 0.012.
Values may be sent and summed in bfloat16 or wider, within the bound.
No kernel may reach another device: no remote copies, remote signals or barrier semaphores. Data moves between devices by JAX's collectives and lax.ppermute only.
A program may use at most 384 MiB of HBM per device.

```python
import jax
import jax.numpy as jnp
from jax import lax

D = 384
HEADS = 6
FF = 1536
E = 8
SEQ = 197
TOP = 2
IMG_DEV = 16
HEAD_DIM = 64
TOK_DEV = 3152
TOKENS = 100864
CAP = 788


def draw_pairs(key):
    key = jax.random.fold_in(key, 11)
    key_shift, key_first, key_second = jax.random.split(key, 3)
    groups = TOKENS // TOK_DEV
    offset = jax.random.randint(key_shift, (groups, 1), 0, E)
    raw = jax.random.randint(key_first, (groups, TOK_DEV), 0, E + 3)
    choose = jnp.where(raw >= E, raw - E, raw)
    forced = (jnp.arange(TOK_DEV) % 4 == 0)[None, :]
    choose = jnp.where(forced, 0, choose)
    first = (choose + offset) % E
    second = (first + jax.random.randint(key_second, (groups, TOK_DEV), 1, E)) % E
    order = jnp.concatenate([first, second], axis=1)
    onehot = (order[:, :, None] == jnp.arange(E)[None, None, :]).astype(jnp.int32)
    ranks = jnp.sum((jnp.cumsum(onehot, axis=1) - 1) * onehot, axis=-1)
    ranks = jnp.minimum(ranks, CAP)
    routes = jnp.stack([first, second], axis=-1).reshape(TOKENS, TOP).astype(jnp.int32)
    slots = jnp.stack([ranks[:, :TOK_DEV], ranks[:, TOK_DEV:]], axis=-1).reshape(TOKENS, TOP).astype(jnp.int32)
    return (routes, slots)


def draw_routes(key, part):
    return draw_pairs(key)[0]


def draw_slots(key, part):
    return draw_pairs(key)[1]


def draw_attn_weights(key, part):
    key = jax.random.fold_in(key, 5)
    entries = jax.random.normal(key, (4 * D, D), jnp.float32) * D ** (-0.5)
    row_ids = jnp.arange(4 * D)[:, None]
    return jnp.where(row_ids >= 3 * D, 3.0 * entries, entries).astype(jnp.bfloat16)


def level_of(rng, shape, cuts, smallest, high):
    def one(axis_at, parts):
        heights = jax.random.uniform(jax.random.fold_in(jax.random.fold_in(rng, 6), axis_at), (parts,), jnp.float32, smallest / len(cuts), high / len(cuts))
        return jnp.repeat(jnp.exp(heights), shape[axis_at] // parts).reshape((-1,) + (1,) * (len(shape) - axis_at - 1))

    level = one(*cuts[0])
    for cut in cuts[1:]:
        level = level * one(*cut)
    return level


def bell_draw(rng, shape, deviation, most, cuts=(), kind=jnp.bfloat16):
    gain = level_of(rng, shape, cuts, -0.22, 0.18) if cuts else 1.0
    drawn = jax.random.normal(rng, shape, jnp.float32) * deviation * gain
    return jnp.minimum(jnp.maximum(drawn, -most), most).astype(kind)


def setup_inputs(seed: int = 0) -> dict:
    arg_keys = jax.random.split(jax.random.key(seed), 11)
    return {
        "tokens": bell_draw(arg_keys[0], (TOKENS, D), 1.0, 6.0, ((0, 32),)),
        "attn_weights": draw_attn_weights(jax.random.fold_in(arg_keys[10], 71), 0),
        "expert_in": bell_draw(arg_keys[2], (E * D, FF), D ** -0.5, 0.3125, ((0, 32),)),
        "expert_out": bell_draw(arg_keys[3], (E * FF, D), (FF // 16) ** -0.5, 0.625, ((0, 32),)),
        "gain_one": jnp.clip(1.0 + 0.1 * jax.random.normal(arg_keys[4], (D,), jnp.float32), 0.5, 1.5),
        "gain_two": jnp.clip(1.0 + 0.1 * jax.random.normal(arg_keys[5], (D,), jnp.float32), 0.5, 1.5),
        "router": bell_draw(arg_keys[6], (D, E), (2 * D) ** -0.5, 0.21875, (), jnp.float32),
        "routes": draw_routes(jax.random.fold_in(arg_keys[10], 71), 0),
        "slots": draw_slots(jax.random.fold_in(arg_keys[10], 71), 0),
        "cotangent": bell_draw(arg_keys[9], (TOKENS, D), 1.0, 6.0, ((0, 32),)),
    }


@jax.custom_vjp
def low(v):
    return lax.optimization_barrier(v.astype(jnp.bfloat16)).astype(jnp.float32)

@jax.custom_vjp
def low_back(v):
    return v

def low_keep(v):
    return (low(v), None)

def low_pass(kept, grad):
    return (grad,)

def back_keep(v):
    return (v, None)

def back_low(kept, grad):
    return (low(grad),)
low.defvjp(low_keep, low_pass)
low_back.defvjp(back_keep, back_low)

def layer_norm(values, scale_gain):
    centred = values - lax.optimization_barrier(jnp.mean(values, axis=-1, keepdims=True))
    spread = lax.optimization_barrier(jnp.mean(centred * centred, axis=-1, keepdims=True))
    return centred * lax.rsqrt(spread + 1e-06) * scale_gain

def route_gates(logit_rows, route_rows):
    chances = jax.nn.softmax(logit_rows, axis=-1)
    picked = route_rows[:, :, None] == jnp.arange(logit_rows.shape[1], dtype=jnp.int32)[None, None, :]
    return lax.optimization_barrier(jnp.sum(jnp.where(picked, chances[:, None, :], 0.0), axis=-1))

def dispatch_tables(route_rows, slot_rows):
    row_count = route_rows.shape[0]
    slot_index = jnp.where(slot_rows < CAP, route_rows * CAP + slot_rows, E * CAP).astype(jnp.int32)
    owners = jnp.broadcast_to(jnp.arange(row_count, dtype=jnp.int32)[:, None], slot_index.shape)
    slot_owner = jnp.full((E * CAP + 1,), row_count, jnp.int32).at[slot_index.reshape(-1)].set(owners.reshape(-1))
    return (slot_owner[:E * CAP], slot_index)

def forward(values, params, route_rows, slot_rows):
    attn_full, in_full, out_full, gain_one, gain_two, router = params
    highest = lax.Precision.HIGHEST
    normed_one = low(layer_norm(values, gain_one))

    def project(weight):
        product = low(low_back(jnp.dot(normed_one, weight, precision=highest)))
        return product.reshape(IMG_DEV, SEQ, HEADS, HEAD_DIM)
    queries = project(attn_full[0:D])
    key_rows = project(attn_full[D:2 * D])
    value_rows = project(attn_full[2 * D:3 * D])
    scores = low_back(jnp.einsum('bqhd,bkhd->bhqk', queries, key_rows, precision=highest) * HEAD_DIM ** (-0.5))
    attn_probs = low(jax.nn.softmax(scores, axis=-1))
    context = low(low_back(jnp.einsum('bhqk,bkhd->bqhd', attn_probs, value_rows, precision=highest)))
    context = context.reshape(TOK_DEV, D)
    residual = values + low_back(jnp.dot(context, attn_full[3 * D:4 * D], precision=highest))
    normed_two = low(layer_norm(residual, gain_two))
    logit_rows = jnp.dot(normed_two, router, precision=highest)
    gate_pair = route_gates(logit_rows, route_rows)
    slot_owner, slot_index = dispatch_tables(route_rows, slot_rows)
    padded = jnp.concatenate([normed_two, jnp.zeros((1, D), normed_two.dtype)], axis=0)
    expert_rows = padded[slot_owner].reshape(E, CAP, D)
    pre_act = low_back(jnp.einsum('ecd,edf->ecf', expert_rows, in_full.reshape(E, D, FF), precision=highest))
    hidden = low(jax.nn.gelu(pre_act, approximate=False))
    returned = low_back(jnp.einsum('ecf,efd->ecd', hidden, out_full.reshape(E, FF, D), precision=highest))
    flat_out = jnp.concatenate([returned.reshape(E * CAP, D), jnp.zeros((1, D), returned.dtype)], axis=0)
    combined = gate_pair[:, 0:1] * flat_out[slot_index[:, 0]] + gate_pair[:, 1:2] * flat_out[slot_index[:, 1]]
    return residual + combined

def reference(tokens, attn_weights, expert_in, expert_out, gain_one, gain_two, router, routes, slots, cotangent):
    weights = (attn_weights.astype(jnp.float32), expert_in.astype(jnp.float32), expert_out.astype(jnp.float32), gain_one, gain_two, router)
    groups = TOKENS // TOK_DEV
    inputs = (tokens.astype(jnp.float32).reshape(groups, TOK_DEV, D), routes.reshape(groups, TOK_DEV, TOP), slots.reshape(groups, TOK_DEV, TOP), cotangent.astype(jnp.float32).reshape(groups, TOK_DEV, D))

    def advance(summed, entry):
        rows_in, route_rows, slot_rows, cot_rows = entry

        def apply_layer(values, *params):
            return forward(values, params, route_rows, slot_rows)
        result, pull_back = jax.vjp(apply_layer, rows_in, *weights)
        gradients = pull_back(cot_rows)
        summed = tuple((earlier + current for earlier, current in zip(summed, gradients[1:])))
        return (summed, (result.astype(jnp.bfloat16), gradients[0].astype(jnp.bfloat16)))
    start = tuple((jnp.zeros(weight.shape, weight.dtype) for weight in weights))
    summed, (results, grad_rows) = lax.scan(advance, start, inputs)
    return (results.reshape(TOKENS, D), grad_rows.reshape(TOKENS, D), summed[0], summed[1], summed[2], summed[3], summed[4], summed[5])
```

```python
import functools

import jax
import jax.numpy as jnp
from jax import lax
from jax.experimental import pallas as pl
from jax.experimental.pallas import tpu as pltpu
from jax.sharding import PartitionSpec as P

D = 384
HEADS = 6
FF = 1536
E = 8
SEQ = 197
IMG = 16
HD = 64
TOK = 3152
CAP = 788
ROWS = 800
CH = 400
NCH = 8
PAD = CH * NCH
QW = 224
KW = 256
ZERO_SLOT = E * ROWS
EPSILON = 1e-06
NEG = -1e30
F32 = jnp.float32
BF16 = jnp.bfloat16
MIB = 1 << 20
SHARDS = 32
SHARD = 4 * D // SHARDS


def dot_nn(a, b):
    return lax.dot_general(a, b, (((1,), (0,)), ((), ())), preferred_element_type=F32)


def dot_nt(a, b):
    return lax.dot_general(a, b, (((1,), (1,)), ((), ())), preferred_element_type=F32)


def dot_tn(a, b):
    return lax.dot_general(a, b, (((0,), (0,)), ((), ())), preferred_element_type=F32)


def params(limit=60):
    return pltpu.CompilerParams(
        dimension_semantics=("arbitrary",), vmem_limit_bytes=limit * MIB
    )


def normalise(values):
    centred = values - jnp.mean(values, axis=-1, keepdims=True)
    spread = jnp.mean(centred * centred, axis=-1, keepdims=True)
    scale = lax.rsqrt(spread + EPSILON)
    return centred * scale, scale


def norm_pull(n, scale, grad, gain):
    h = grad * gain
    return scale * (
        h - jnp.mean(h, axis=-1, keepdims=True) - n * jnp.mean(h * n, axis=-1, keepdims=True)
    )


def row_mask(step, rows, limit):
    ids = lax.broadcasted_iota(jnp.int32, (rows, 1), 0) + step * rows
    return ids < limit


def whole(shape):
    zeros = (0,) * len(shape)
    return pl.BlockSpec(shape, lambda *_: zeros, pipeline_mode=pl.Buffered(1))


def owners_kernel(idx_ref, out_ref):
    def clear(i, carry):
        for u in range(16):
            out_ref[i * 16 + u] = jnp.int32(PAD)
        return carry

    lax.fori_loop(0, (ZERO_SLOT + 16) // 16, clear, 0)

    def put(i, carry):
        for u in range(8):
            t = i * 8 + u
            out_ref[idx_ref[0, t]] = t
            out_ref[idx_ref[1, t]] = t
        return carry

    lax.fori_loop(0, TOK // 8, put, 0)


def slot_owners(idx):
    return pl.pallas_call(
        owners_kernel,
        out_shape=jax.ShapeDtypeStruct((ZERO_SLOT + 16,), jnp.int32),
        in_specs=[pl.BlockSpec(memory_space=pltpu.SMEM)],
        out_specs=pl.BlockSpec(memory_space=pltpu.SMEM),
        name="slot_owners",
    )(idx)


def project_kernel(at_ref, tok_ref, rel_ref, gain_ref, qkv_ref, w_ref):
    step = pl.program_id(0)

    @pl.when(step == 0)
    def _():
        x, y, core, z = at_ref[0], at_ref[1], at_ref[2], at_ref[3]
        for b in range(SHARDS):
            zb, yb, xb, cb = b // 8, (b // 4) % 2, (b // 2) % 2, b % 2
            j = (cb ^ core) * 16 + (yb ^ y) * 8 + (xb ^ x) * 4 + (zb ^ z)
            w_ref[b * SHARD : (b + 1) * SHARD, :] = rel_ref[j]

    values = jnp.where(row_mask(step, CH, TOK), tok_ref[...].astype(F32), 0.0)
    n, _ = normalise(values)
    normed = (n * gain_ref[...]).astype(BF16)
    for b in range(3):
        cols = dot_nn(normed, w_ref[b * D : (b + 1) * D, :])
        qkv_ref[:, b * D : (b + 1) * D] = cols.astype(BF16)


def project(at, tokens, relative, gain):
    return pl.pallas_call(
        project_kernel,
        grid_spec=pltpu.PrefetchScalarGridSpec(
            num_scalar_prefetch=1,
            grid=(NCH,),
            in_specs=[
                pl.BlockSpec((CH, D), lambda i, a: (i, 0)),
                whole((SHARDS, SHARD, D)),
                whole((1, D)),
            ],
            out_specs=(
                pl.BlockSpec((CH, 3 * D), lambda i, a: (i, 0)),
                whole((4 * D, D)),
            ),
        ),
        out_shape=(
            jax.ShapeDtypeStruct((PAD, 3 * D), BF16),
            jax.ShapeDtypeStruct((4 * D, D), BF16),
        ),
        compiler_params=params(),
        cost_estimate=pl.CostEstimate(flops=2 * TOK * D * D * 3, bytes_accessed=12 * MIB, transcendentals=0),
        name="project",
    )(at, tokens, relative, gain)


def window(image):
    start = image * SEQ
    base = pl.multiple_of((start // 16) * 16, 16)
    return base, start - base


def attend_kernel(qkv_ref, ctx_ref, probs_ref):
    image = pl.program_id(0)
    base, off = window(image)
    keys = lax.broadcasted_iota(jnp.int32, (1, KW), 1)
    key_ok = jnp.logical_and(keys >= off, keys < off + SEQ)
    rows = lax.broadcasted_iota(jnp.int32, (QW, 1), 0)
    row_ok = jnp.logical_and(rows >= off, rows < off + SEQ)
    lanes = lax.broadcasted_iota(jnp.int32, (1, 128), 1)
    for pair in range(HEADS // 2):
        cols = pl.ds(pair * 128, 128)
        q = qkv_ref[pl.ds(base, QW), cols]
        k = qkv_ref[pl.ds(base, KW), pl.ds(D + pair * 128, 128)]
        v = qkv_ref[pl.ds(base, KW), pl.ds(2 * D + pair * 128, 128)]
        total = jnp.zeros((QW, 128), F32)
        for half in range(2):
            mine = jnp.logical_and(lanes >= half * HD, lanes < (half + 1) * HD)
            qh = jnp.where(mine, q, jnp.zeros_like(q))
            vh = jnp.where(mine, v, jnp.zeros_like(v))
            scores = dot_nt(qh, k) * HD ** (-0.5)
            scores = jnp.where(key_ok, scores, NEG)
            top = jnp.max(scores, axis=-1, keepdims=True)
            raw = jnp.exp(scores - top)
            probs = (raw * (1.0 / jnp.sum(raw, axis=-1, keepdims=True))).astype(BF16)
            probs_ref[0, pair * 2 + half] = probs
            total = total + dot_nn(probs, vh)
        old = ctx_ref[pl.ds(base, QW), cols]
        ctx_ref[pl.ds(base, QW), cols] = jnp.where(row_ok, total.astype(BF16), old)


def attend(qkv):
    return pl.pallas_call(
        attend_kernel,
        grid=(IMG,),
        out_shape=(
            jax.ShapeDtypeStruct((PAD, D), BF16),
            jax.ShapeDtypeStruct((IMG, HEADS, QW, KW), BF16),
        ),
        in_specs=[whole((PAD, 3 * D))],
        out_specs=(
            pl.BlockSpec((PAD, D), lambda i: (0, 0), pipeline_mode=pl.Buffered(1)),
            pl.BlockSpec((1, HEADS, QW, KW), lambda i: (i, 0, 0, 0)),
        ),
        compiler_params=params(),
        cost_estimate=pl.CostEstimate(flops=IMG * HEADS * QW * KW * 512, bytes_accessed=24 * MIB, transcendentals=0),
        name="attend",
    )(qkv)


def dispatch_kernel(
    owner_ref, ctx_ref, tok_ref, cot_ref, w_ref, gain_ref, rhi_ref, rlo_ref,
    res_ref, chance_ref, xg_ref, pg_ref, table, picked,
):
    step = pl.program_id(0)
    lanes = lax.broadcasted_iota(jnp.int32, (1, 128), 1)

    @pl.when(step == 0)
    def _():
        table[pl.ds(PAD * 8, 8), :] = jnp.zeros((8, 128), F32)

    @pl.when(step < NCH)
    def _():
        residual = tok_ref[...].astype(F32) + dot_nn(ctx_ref[...], w_ref[...])
        res_ref[...] = residual
        n, _ = normalise(residual)
        normed = (n * gain_ref[...]).astype(BF16)
        logits = dot_nn(normed, rhi_ref[...]) + dot_nn(normed, rlo_ref[...])
        logits = jnp.where(lanes < E, logits, NEG)
        raw = jnp.exp(logits - jnp.max(logits, axis=-1, keepdims=True))
        chances = raw / jnp.sum(raw, axis=-1, keepdims=True)
        chance_ref[...] = chances
        wide = normed.astype(F32)
        cot = cot_ref[...].astype(F32)
        at = pl.multiple_of(step * CH * 8, 8)
        for j in range(3):
            part = slice(j * 128, (j + 1) * 128)
            table[pl.ds(at + j, CH, stride=8), :] = wide[:, part]
            table[pl.ds(at + 3 + j, CH, stride=8), :] = cot[:, part]
        table[pl.ds(at + 6, CH, stride=8), :] = chances

    @pl.when(step >= NCH)
    def _():
        first = (step - NCH) * ROWS

        def pick(i, carry):
            for u in range(32):
                c = i * 32 + u
                row = pl.multiple_of(owner_ref[first + c] * 8, 8)
                picked[pl.ds(pl.multiple_of(c * 8, 8), 8), :] = table[pl.ds(row, 8), :]
            return carry

        lax.fori_loop(0, ROWS // 32, pick, 0)
        for j in range(6):
            xg_ref[0, :, j * 128 : (j + 1) * 128] = picked[pl.ds(j, ROWS, stride=8), :].astype(BF16)
        pg_ref[0] = picked[pl.ds(6, ROWS, stride=8), :]


def dispatch(owner, ctx, tokens, cotangent, weights, gain, rhi, rlo):
    chunk = lambda i, o: (jnp.minimum(i, NCH - 1), 0)
    expert = lambda i, o: (jnp.maximum(i - NCH, 0), 0, 0)
    full = lambda shape: pl.BlockSpec(shape, lambda i, o: (0,) * len(shape), pipeline_mode=pl.Buffered(1))
    return pl.pallas_call(
        dispatch_kernel,
        grid_spec=pltpu.PrefetchScalarGridSpec(
            num_scalar_prefetch=1,
            grid=(NCH + E,),
            in_specs=[
                pl.BlockSpec((CH, D), chunk),
                pl.BlockSpec((CH, D), chunk),
                pl.BlockSpec((CH, D), chunk),
                pl.BlockSpec((D, D), lambda i, o: (3, 0), pipeline_mode=pl.Buffered(1)),
                full((1, D)),
                full((D, 128)),
                full((D, 128)),
            ],
            out_specs=(
                pl.BlockSpec((CH, D), chunk),
                pl.BlockSpec((CH, 128), chunk),
                pl.BlockSpec((1, ROWS, 2 * D), expert),
                pl.BlockSpec((1, ROWS, 128), expert),
            ),
            scratch_shapes=[
                pltpu.VMEM(((PAD + 1) * 8, 128), F32),
                pltpu.VMEM((ROWS * 8, 128), F32),
            ],
        ),
        out_shape=(
            jax.ShapeDtypeStruct((TOK, D), F32),
            jax.ShapeDtypeStruct((TOK, 128), F32),
            jax.ShapeDtypeStruct((E, ROWS, 2 * D), BF16),
            jax.ShapeDtypeStruct((E, ROWS, 128), F32),
        ),
        compiler_params=params(),
        cost_estimate=pl.CostEstimate(flops=2 * TOK * D * D * 10, bytes_accessed=30 * MIB, transcendentals=0),
        name="dispatch",
    )(owner, ctx, tokens, cotangent, weights, gain, rhi, rlo)


A1, A2, A3, A4, A5 = (
    0.5 * 0.254829592, 0.5 * -0.284496736, 0.5 * 1.421413741, 0.5 * -1.453152027, 0.5 * 1.061405429
)


def gelu_parts(u):
    t = 1.0 / (1.0 + (0.3275911 * 0.5**0.5) * jnp.abs(u))
    bell = jnp.exp(-0.5 * (u * u))
    tail = ((((A5 * t + A4) * t + A3) * t + A2) * t + A1) * t * bell
    cdf = jnp.where(u < 0, tail, 1.0 - tail)
    return u * cdf, cdf + u * (bell * 0.3989422804014327)


def expert_kernel(far, at_ref, xg_ref, pg_ref, *refs):
    win, wout = refs[0:8], refs[8:16]
    y_ref, gg_ref = refs[16:18]
    gwin, gwout = refs[18:26], refs[26:34]
    win_s, wout_s, gwin_s, xt_s, gt_s, g_s, ret_s, gr_s = refs[34:]
    step = pl.program_id(0)
    x, y, core, z = at_ref[0], at_ref[1], at_ref[2], at_ref[3]
    rel_y = step % 2
    expert = 2 * ((2 * far + step // 2) ^ z) + (rel_y ^ y)
    place = [((r // 2) ^ x) * 2 + ((r % 2) ^ core) for r in range(4)]
    for side in range(2):

        @pl.when(rel_y == side)
        def _():
            for r in range(4):
                rows = pl.ds(pl.multiple_of(place[r] * 96, 16), 96)
                win_s[rows, :] = win[side * 4 + r][0]
                wout_s[r] = wout[side * 4 + r][0]

    lanes = lax.broadcasted_iota(jnp.int32, (1, 128), 1)
    gate = jnp.sum(jnp.where(lanes == expert, pg_ref[0], 0.0), axis=-1, keepdims=True)
    g_s[...] = (gate * xg_ref[0, :, D:].astype(F32)).astype(BF16)
    xt_s[...] = xg_ref[0, :, :D].T
    gt_s[...] = g_s[...].T
    parts = []
    for r in range(4):
        cols = pl.ds(pl.multiple_of(place[r] * D, 128), D)
        pre = dot_nn(xg_ref[0, :, :D], win_s[:, cols])
        grad_hidden = dot_nt(g_s[...], wout_s[r])
        value, slope = gelu_parts(pre)
        hidden = value.astype(BF16)
        grad_pre = (grad_hidden * slope).astype(BF16)
        ret = dot_nn(hidden, wout_s[r])
        back = dot_nt(grad_pre, win_s[:, cols])
        if r == 0:
            ret_s[...] = ret
            gr_s[...] = back
        else:
            ret_s[...] += ret
            gr_s[...] += back
        parts.append(dot_nn(gt_s[...], hidden).astype(BF16))
        gwin_s[:, cols] = dot_nn(xt_s[...], grad_pre).astype(BF16)
    ret = ret_s[...]
    y_ref[0, :, :D] = (gate * ret).astype(BF16)
    y_ref[0, :, D:] = gr_s[...].astype(BF16)
    grad_gate = jnp.sum(xg_ref[0, :, D:].astype(F32) * ret, axis=-1, keepdims=True)
    gg_ref[0] = jnp.where(lanes == expert, grad_gate, 0.0)
    for side in range(2):

        @pl.when(rel_y == side)
        def _():
            for r in range(4):
                rows = pl.ds(pl.multiple_of(place[r] * 96, 16), 96)
                gwin[side * 4 + r][0] = gwin_s[rows, :]
                gwout[side * 4 + r][0] = parts[r]


def experts(far, at, xg, pg, win, wout):
    group = E // 2
    mine = lambda s, a: (2 * ((2 * far + s // 2) ^ a[3]) + ((s % 2) ^ a[1]), 0, 0)
    step = lambda s, a: (s, 0, 0)
    half = lambda s, a: (s // 2, 0, 0)
    rows_in = D // 4
    return pl.pallas_call(
        functools.partial(expert_kernel, far),
        grid_spec=pltpu.PrefetchScalarGridSpec(
            num_scalar_prefetch=1,
            grid=(group,),
            in_specs=[pl.BlockSpec((1, ROWS, 2 * D), mine), pl.BlockSpec((1, ROWS, 128), mine)]
            + [pl.BlockSpec((1, rows_in, FF), half)] * 8
            + [pl.BlockSpec((1, D, D), half)] * 8,
            out_specs=[pl.BlockSpec((1, ROWS, 2 * D), step), pl.BlockSpec((1, ROWS, 128), step)]
            + [pl.BlockSpec((1, rows_in, FF), half)] * 8
            + [pl.BlockSpec((1, D, D), half)] * 8,
            scratch_shapes=[
                pltpu.VMEM((D, FF), BF16),
                pltpu.VMEM((4, D, D), BF16),
                pltpu.VMEM((D, FF), BF16),
                pltpu.VMEM((D, ROWS), BF16),
                pltpu.VMEM((D, ROWS), BF16),
                pltpu.VMEM((ROWS, D), BF16),
                pltpu.VMEM((ROWS, D), F32),
                pltpu.VMEM((ROWS, D), F32),
            ],
        ),
        out_shape=[
            jax.ShapeDtypeStruct((group, ROWS, 2 * D), BF16),
            jax.ShapeDtypeStruct((group, ROWS, 128), F32),
        ]
        + [jax.ShapeDtypeStruct((group // 2, rows_in, FF), BF16)] * 8
        + [jax.ShapeDtypeStruct((group // 2, D, D), BF16)] * 8,
        compiler_params=params(),
        cost_estimate=pl.CostEstimate(flops=group * 12 * ROWS * D * FF, bytes_accessed=40 * MIB, transcendentals=0),
        name="experts",
    )(at, xg, pg, *win, *wout)


def combine_kernel(
    at_ref, idx_ref, y0_ref, y1_ref, gg0_ref, gg1_ref, res_ref, cot_ref, chance_ref, ctx_ref,
    w_ref, gain_ref, rhi_ref, rlo_ref,
    out_ref, gres_ref, gctx_ref, gwo_ref, ggain_ref, grouter_ref, table, summed,
):
    step = pl.program_id(0)
    group = E // 2

    @pl.when(step == 0)
    def _():
        table[pl.ds(ZERO_SLOT * 8, 8), :] = jnp.zeros((8, 128), F32)

    for rel in range(2):
        y_ref, gg_ref = ((y0_ref, gg0_ref), (y1_ref, gg1_ref))[rel]

        @pl.when(jnp.logical_and(step >= rel * group, step < (rel + 1) * group))
        def _():
            s = step - rel * group
            expert = 2 * ((2 * rel + s // 2) ^ at_ref[3]) + ((s % 2) ^ at_ref[1])
            to = pl.multiple_of(expert * (ROWS * 8), 8)
            for j in range(6):
                table[pl.ds(to + j, ROWS, stride=8), :] = y_ref[0, :, j * 128 : (j + 1) * 128].astype(F32)
            table[pl.ds(to + 6, ROWS, stride=8), :] = gg_ref[0]

    @pl.when(step >= E)
    def _():
        part = step - E
        first = part * CH

        def add(i, carry):
            for u in range(16):
                c = i * 16 + u
                one = pl.multiple_of(idx_ref[0, first + c] * 8, 8)
                two = pl.multiple_of(idx_ref[1, first + c] * 8, 8)
                summed[pl.ds(pl.multiple_of(c * 8, 8), 8), :] = table[pl.ds(one, 8), :] + table[pl.ds(two, 8), :]
            return carry

        lax.fori_loop(0, CH // 16, add, 0)
        ok = row_mask(part, CH, TOK)
        residual = jnp.where(ok, res_ref[...], 0.0)
        cot = jnp.where(ok, cot_ref[...].astype(F32), 0.0)
        chances = jnp.where(ok, chance_ref[...], 0.0)
        ctx = ctx_ref[...]
        ctx = jnp.where(ok, ctx, jnp.zeros_like(ctx))
        pieces = [summed[pl.ds(j, CH, stride=8), :] for j in range(7)]
        out_ref[...] = (residual + jnp.concatenate(pieces[0:3], axis=-1)).astype(BF16)
        grad_chances = pieces[6]
        grad_logits = chances * (
            grad_chances - jnp.sum(grad_chances * chances, axis=-1, keepdims=True)
        )
        high = grad_logits.astype(BF16)
        rest = (grad_logits - high.astype(F32)).astype(BF16)
        grad_normed = jnp.concatenate(pieces[3:6], axis=-1) + (
            dot_nt(high, rhi_ref[...]) + dot_nt(high, rlo_ref[...]) + dot_nt(rest, rhi_ref[...])
        )
        n, scale = normalise(residual)
        gain = gain_ref[...]
        normed = (n * gain).astype(BF16)
        grad_residual = cot + norm_pull(n, scale, grad_normed, gain)
        gres_ref[...] = grad_residual
        branch = jnp.where(ok, grad_residual, 0.0).astype(BF16)
        gctx_ref[...] = dot_nt(branch, w_ref[...]).astype(BF16)
        gwo = dot_tn(ctx, branch)
        ggain = jnp.sum(jnp.where(ok, grad_normed * n, 0.0), axis=0, keepdims=True)
        grouter = dot_tn(normed, high) + dot_tn(normed, rest)

        @pl.when(part == 0)
        def _():
            gwo_ref[...] = gwo
            ggain_ref[...] = ggain
            grouter_ref[...] = grouter

        @pl.when(part > 0)
        def _():
            gwo_ref[...] += gwo
            ggain_ref[...] += ggain
            grouter_ref[...] += grouter


def combine(at, idx, y0, y1, gg0, gg1, res, cot, chances, ctx, weights, gain, rhi, rlo):
    group = E // 2
    chunk = lambda i, *_: (jnp.maximum(i - E, 0), 0)
    full = lambda shape: pl.BlockSpec(shape, lambda i, *_: (0,) * len(shape), pipeline_mode=pl.Buffered(1))
    early = lambda i, *_: (jnp.minimum(i, group - 1), 0, 0)
    late = lambda i, *_: (jnp.clip(i - group, 0, group - 1), 0, 0)
    fixed = lambda shape: pl.BlockSpec(shape, lambda i, *_: (0,) * len(shape))
    return pl.pallas_call(
        combine_kernel,
        grid_spec=pltpu.PrefetchScalarGridSpec(
            num_scalar_prefetch=2,
            grid=(E + NCH,),
            in_specs=[
                pl.BlockSpec((1, ROWS, 2 * D), early),
                pl.BlockSpec((1, ROWS, 2 * D), late),
                pl.BlockSpec((1, ROWS, 128), early),
                pl.BlockSpec((1, ROWS, 128), late),
                pl.BlockSpec((CH, D), chunk),
                pl.BlockSpec((CH, D), chunk),
                pl.BlockSpec((CH, 128), chunk),
                pl.BlockSpec((CH, D), chunk),
                pl.BlockSpec((D, D), lambda i, *_: (3, 0), pipeline_mode=pl.Buffered(1)),
                full((1, D)),
                full((D, 128)),
                full((D, 128)),
            ],
            out_specs=(
                pl.BlockSpec((CH, D), chunk),
                pl.BlockSpec((CH, D), chunk),
                pl.BlockSpec((CH, D), chunk),
                fixed((D, D)),
                fixed((1, D)),
                fixed((D, 128)),
            ),
            scratch_shapes=[
                pltpu.VMEM(((ZERO_SLOT + 1) * 8, 128), F32),
                pltpu.VMEM((CH * 8, 128), F32),
            ],
        ),
        out_shape=(
            jax.ShapeDtypeStruct((TOK, D), BF16),
            jax.ShapeDtypeStruct((TOK, D), F32),
            jax.ShapeDtypeStruct((PAD, D), BF16),
            jax.ShapeDtypeStruct((D, D), F32),
            jax.ShapeDtypeStruct((1, D), F32),
            jax.ShapeDtypeStruct((D, 128), F32),
        ),
        compiler_params=params(),
        cost_estimate=pl.CostEstimate(flops=2 * TOK * D * D * 10, bytes_accessed=36 * MIB, transcendentals=0),
        name="combine",
    )(at, idx, y0, y1, gg0, gg1, res, cot, chances, ctx, weights, gain, rhi, rlo)


def attend_back_kernel(qkv_ref, ctx_ref, gctx_ref, probs_ref, gqkv_ref):
    image = pl.program_id(0)
    base, off = window(image)
    rows = lax.broadcasted_iota(jnp.int32, (QW, 1), 0)
    row_ok = jnp.logical_and(rows >= off, rows < off + SEQ)
    wide = lax.broadcasted_iota(jnp.int32, (KW, 1), 0)
    wide_ok = jnp.logical_and(wide >= off, wide < off + SEQ)
    lanes = lax.broadcasted_iota(jnp.int32, (1, 128), 1)
    scale = HD ** (-0.5)
    for pair in range(HEADS // 2):
        cols = pl.ds(pair * 128, 128)
        cols_k = pl.ds(D + pair * 128, 128)
        cols_v = pl.ds(2 * D + pair * 128, 128)
        q = qkv_ref[pl.ds(base, QW), cols]
        k = qkv_ref[pl.ds(base, KW), cols_k]
        v = qkv_ref[pl.ds(base, KW), cols_v]
        grad = gctx_ref[pl.ds(base, QW), cols]
        grad = jnp.where(row_ok, grad, jnp.zeros_like(grad))
        ctx = ctx_ref[pl.ds(base, QW), cols]
        product = grad.astype(F32) * jnp.where(row_ok, ctx, jnp.zeros_like(ctx)).astype(F32)
        gq = jnp.zeros((QW, 128), F32)
        gk = jnp.zeros((KW, 128), F32)
        gv = jnp.zeros((KW, 128), F32)
        for half in range(2):
            mine = jnp.logical_and(lanes >= half * HD, lanes < (half + 1) * HD)
            grad_h = jnp.where(mine, grad, jnp.zeros_like(grad))
            q_h = jnp.where(mine, q, jnp.zeros_like(q))
            k_h = jnp.where(mine, k, jnp.zeros_like(k))
            mean = jnp.sum(jnp.where(mine, product, 0.0), axis=-1, keepdims=True)
            probs = probs_ref[0, pair * 2 + half]
            grad_probs = dot_nt(grad_h, v)
            grad_scores = (probs.astype(F32) * (grad_probs - mean)).astype(BF16)
            gv = gv + dot_tn(probs, grad_h)
            gq = gq + dot_nn(grad_scores, k_h)
            gk = gk + dot_tn(grad_scores, q_h)
        old = gqkv_ref[pl.ds(base, QW), cols]
        gqkv_ref[pl.ds(base, QW), cols] = jnp.where(row_ok, (gq * scale).astype(BF16), old)
        old = gqkv_ref[pl.ds(base, KW), cols_k]
        gqkv_ref[pl.ds(base, KW), cols_k] = jnp.where(wide_ok, (gk * scale).astype(BF16), old)
        old = gqkv_ref[pl.ds(base, KW), cols_v]
        gqkv_ref[pl.ds(base, KW), cols_v] = jnp.where(wide_ok, gv.astype(BF16), old)


def attend_back(qkv, ctx, gctx, probs):
    return pl.pallas_call(
        attend_back_kernel,
        grid=(IMG,),
        out_shape=jax.ShapeDtypeStruct((PAD, 3 * D), BF16),
        in_specs=[
            whole((PAD, 3 * D)),
            whole((PAD, D)),
            whole((PAD, D)),
            pl.BlockSpec((1, HEADS, QW, KW), lambda i: (i, 0, 0, 0)),
        ],
        out_specs=pl.BlockSpec((PAD, 3 * D), lambda i: (0, 0), pipeline_mode=pl.Buffered(1)),
        compiler_params=params(),
        cost_estimate=pl.CostEstimate(flops=IMG * HEADS * QW * KW * 1024, bytes_accessed=40 * MIB, transcendentals=0),
        name="attend_back",
    )(qkv, ctx, gctx, probs)


def finish_kernel(
    at_ref, tok_ref, gqkv_ref, gres_ref, w_ref, gain_ref, gwo_ref, gtok_ref, rel_ref, ggain_ref, gw_s
):
    step = pl.program_id(0)
    ok = row_mask(step, CH, TOK)
    values = jnp.where(ok, tok_ref[...].astype(F32), 0.0)
    n, scale = normalise(values)
    gain = gain_ref[...]
    normed = (n * gain).astype(BF16)
    gqkv = gqkv_ref[...]
    gqkv = jnp.where(ok, gqkv, jnp.zeros_like(gqkv))
    grad = dot_nt(gqkv[:, 0:D], w_ref[0:D, :])
    for b in range(1, 3):
        grad = grad + dot_nt(gqkv[:, b * D : (b + 1) * D], w_ref[b * D : (b + 1) * D, :])
    gtok_ref[...] = (gres_ref[...] + norm_pull(n, scale, grad, gain)).astype(BF16)
    ggain = jnp.sum(grad * n, axis=0, keepdims=True)
    gw = dot_tn(normed, gqkv)

    @pl.when(step == 0)
    def _():
        gw_s[...] = gw
        ggain_ref[...] = ggain

    @pl.when(step > 0)
    def _():
        gw_s[...] += gw
        ggain_ref[...] += ggain

    @pl.when(step == NCH - 1)
    def _():
        x, y, core, z = at_ref[0], at_ref[1], at_ref[2], at_ref[3]
        for b in range(SHARDS):
            zb, yb, xb, cb = b // 8, (b // 4) % 2, (b // 2) % 2, b % 2
            j = (cb ^ core) * 16 + (yb ^ y) * 8 + (xb ^ x) * 4 + (zb ^ z)
            rows = slice((b % 8) * SHARD, (b % 8 + 1) * SHARD)
            part = gwo_ref[rows, :] if zb == 3 else gw_s[rows, zb * D : (zb + 1) * D]
            rel_ref[j] = part.astype(BF16)


def finish(at, tokens, gqkv, gres, weights, gain, gwo):
    chunk = lambda i, a: (i, 0)
    return pl.pallas_call(
        finish_kernel,
        grid_spec=pltpu.PrefetchScalarGridSpec(
            num_scalar_prefetch=1,
            grid=(NCH,),
            in_specs=[
                pl.BlockSpec((CH, D), chunk),
                pl.BlockSpec((CH, 3 * D), chunk),
                pl.BlockSpec((CH, D), chunk),
                whole((4 * D, D)),
                whole((1, D)),
                whole((D, D)),
            ],
            out_specs=(
                pl.BlockSpec((CH, D), chunk),
                whole((SHARDS, SHARD, D)),
                pl.BlockSpec((1, D), lambda i, a: (0, 0)),
            ),
            scratch_shapes=[pltpu.VMEM((D, 3 * D), F32)],
        ),
        out_shape=(
            jax.ShapeDtypeStruct((TOK, D), BF16),
            jax.ShapeDtypeStruct((SHARDS, SHARD, D), BF16),
            jax.ShapeDtypeStruct((1, D), F32),
        ),
        compiler_params=params(),
        cost_estimate=pl.CostEstimate(flops=2 * TOK * D * D * 6, bytes_accessed=20 * MIB, transcendentals=0),
        name="finish",
    )(at, tokens, gqkv, gres, weights, gain, gwo)


def trade(value, bit, n):
    return lax.ppermute(value, "dp", [(i, i ^ bit) for i in range(n)])


def gather_attn(own, n):
    rel_z = jnp.stack([own] + [trade(own, 8 * j, n) for j in (1, 2, 3)])
    rel_xy = jnp.concatenate([rel_z] + [trade(rel_z, 2 * j, n) for j in (1, 2, 3)])
    return jnp.concatenate([rel_xy, trade(rel_xy, 1, n)])


def gather_group(pair, n):
    from_x = trade(pair, 2, n)
    from_y = trade(pair, 4, n)
    corner = jnp.concatenate([trade(from_x[0:1], 4, n), trade(from_y[1:2], 2, n)])
    gathered = []
    for part in (pair, from_x, from_y, corner):
        gathered += [part, trade(part, 1, n)]
    return gathered


def add_low(*parts):
    total = parts[0].astype(F32)
    for part in parts[1:]:
        total = total + part.astype(F32)
    return total.astype(BF16)


def scatter_group(grads, n):
    near, along_x, along_y, corner = (
        add_low(grads[2 * i], trade(grads[2 * i + 1], 1, n)) for i in range(4)
    )
    via_x = trade(corner[0:1], 2, n)
    via_y = trade(corner[1:2], 4, n)
    along_y = jnp.concatenate([add_low(along_y[0:1], via_x), along_y[1:2]])
    along_x = jnp.concatenate([along_x[0:1], add_low(along_x[1:2], via_y)])
    return add_low(near, trade(along_x, 2, n), trade(along_y, 4, n))


def scatter_z(first, second, n):
    one = trade(first[1], 8, n)
    two = trade(second[0], 16, n)
    three = trade(second[1], 24, n)
    return (first[0].astype(F32) + one.astype(F32)) + (two.astype(F32) + three.astype(F32))


def scatter_attn(rel, n):
    both = add_low(rel[:16], trade(rel[16:], 1, n)).reshape(4, 4, SHARD, D)
    own = add_low(both[0], *[trade(both[j], 2 * j, n) for j in (1, 2, 3)])
    parts = [trade(own[j], 8 * j, n).astype(F32) for j in (1, 2, 3)]
    return (own[0].astype(F32) + parts[0]) + (parts[1] + parts[2])


def sum_all(value, n):
    value = value + trade(value, 1, n)
    value = (value + trade(value, 2, n)) + (trade(value, 4, n) + trade(value, 6, n))
    return (value + trade(value, 8, n)) + (trade(value, 16, n) + trade(value, 24, n))


def split_groups(full, rows):
    parts = full.reshape(4, 2, 2, 2, rows, full.shape[-1])
    return [
        [parts[2 * g : 2 * g + 2, r // 4, (r // 2) % 2, r % 2] for r in range(8)] for g in range(2)
    ]


def join_groups(groups):
    rows, columns = groups[0][0].shape[1:]
    whole_z = [jnp.concatenate([groups[0][r], groups[1][r]]) for r in range(8)]
    return jnp.stack(whole_z, axis=1).reshape(SHARDS, rows, columns)


def on_device(
    n, tokens, attn_weights, expert_in, expert_out, gain_one, gain_two, router, routes, slots,
    cotangent,
):
    placed = n == SHARDS
    if placed:
        me = lax.axis_index("dp")
        at = jnp.stack([(me >> 1) & 1, (me >> 2) & 1, me & 1, me >> 3]).astype(jnp.int32)
        relative = gather_attn(attn_weights, n)
        win, wout = [], []
        for own, into in ((expert_in, win), (expert_out, wout)):
            into.append(gather_group(jnp.stack([own, trade(own, 8, n)]), n))
            into.append(gather_group(jnp.stack([trade(own, 16, n), trade(own, 24, n)]), n))
    else:
        at = jnp.zeros((4,), jnp.int32)
        full = lax.all_gather(attn_weights, "dp", axis=0, tiled=True)
        full = full.reshape(4, 2, 2, 2, SHARD, D)
        relative = full.transpose(3, 1, 2, 0, 4, 5).reshape(SHARDS, SHARD, D)
        win = split_groups(lax.all_gather(expert_in, "dp", axis=0, tiled=True), D // 4)
        wout = split_groups(lax.all_gather(expert_out, "dp", axis=0, tiled=True), D)
    idx = jnp.where(slots < CAP, routes * ROWS + slots, ZERO_SLOT).astype(jnp.int32).T
    idx_pad = jnp.pad(idx, ((0, 0), (0, PAD - TOK)), constant_values=ZERO_SLOT)
    owner = slot_owners(idx)
    wide = jnp.pad(router, ((0, 0), (0, 128 - E)))
    rhi = wide.astype(BF16)
    rlo = (wide - rhi.astype(F32)).astype(BF16)
    one = gain_one.reshape(1, D)
    two = gain_two.reshape(1, D)
    qkv, weights = project(at, tokens, relative, one)
    ctx, probs = attend(qkv)
    res, chances, xg, pg = dispatch(owner, ctx, tokens, cotangent, weights, two, rhi, rlo)
    group = [experts(far, at, xg, pg, win[far], wout[far]) for far in range(2)]
    out, gres, gctx, gwo, ggain_two, grouter = combine(
        at, idx_pad, group[0][0], group[1][0], group[0][1], group[1][1],
        res, cotangent, chances, ctx, weights, two, rhi, rlo,
    )
    gqkv = attend_back(qkv, ctx, gctx, probs)
    gtok, grel, ggain_one = finish(at, tokens, gqkv, gres, weights, one, gwo)
    small = jnp.concatenate([ggain_one, ggain_two, grouter[:, :E].reshape(E, D)])
    if placed:
        gin = scatter_z(*(scatter_group(g[2:10], n) for g in group), n)
        gout = scatter_z(*(scatter_group(g[10:18], n) for g in group), n)
        gattn = scatter_attn(grel, n)
        small = sum_all(small, n)
        gout = gout.T
    else:
        gin = join_groups([g[2:10] for g in group]).reshape(E * D, FF)
        gout = jnp.swapaxes(join_groups([g[10:18] for g in group]), -1, -2).reshape(E * FF, D)
        gattn = grel.reshape(2, 2, 2, 4, SHARD, D).transpose(3, 1, 2, 0, 4, 5).reshape(4 * D, D)
        gin, gout, gattn = (
            lax.psum_scatter(g.astype(F32), "dp", scatter_dimension=0, tiled=True)
            for g in (gin, gout, gattn)
        )
        small = lax.psum(small, "dp")
    return out, gtok, gattn, gin, gout, small[0], small[1], small[2:].reshape(D, E)


def solution(mesh):
    split = P("dp", None)
    return jax.shard_map(
        functools.partial(on_device, mesh.shape["dp"]),
        mesh=mesh,
        in_specs=(split, split, split, split, P(), P(), P(), split, split, split),
        out_specs=(split, split, split, split, split, P(), P(), P()),
        check_vma=False,
    )
```

```python
import functools

import jax
import jax.numpy as jnp
from jax import lax
from jax.experimental import pallas as pl
from jax.experimental.pallas import tpu as pltpu
from jax.sharding import PartitionSpec as P

D = 384
HEADS = 6
FF = 1536
E = 8
SEQ = 197
IMG = 16
HD = 64
TOK = 3152
CAP = 788
ROWS = 800
CH = 800
NCH = 4
PAD = CH * NCH
QW = 224
KW = 256
ZERO_SLOT = E * ROWS
EPSILON = 1e-06
NEG = -1e30
HALF = IMG // 2
FCH = 256
ORDER = ((1, 0), (1, 1), (0, 1), (0, 0))
F32 = jnp.float32
BF16 = jnp.bfloat16
MIB = 1 << 20
SHARDS = 32
SHARD = 4 * D // SHARDS


def dot_nn(a, b):
    return lax.dot_general(a, b, (((1,), (0,)), ((), ())), preferred_element_type=F32)


def dot_nt(a, b):
    return lax.dot_general(a, b, (((1,), (1,)), ((), ())), preferred_element_type=F32)


def dot_tn(a, b):
    return lax.dot_general(a, b, (((0,), (0,)), ((), ())), preferred_element_type=F32)


def params(limit=60):
    return pltpu.CompilerParams(
        dimension_semantics=("arbitrary",), vmem_limit_bytes=limit * MIB
    )


def normalise(values):
    centred = values - jnp.mean(values, axis=-1, keepdims=True)
    spread = jnp.mean(centred * centred, axis=-1, keepdims=True)
    scale = lax.rsqrt(spread + EPSILON)
    return centred * scale, scale


def norm_pull(n, scale, grad, gain):
    h = grad * gain
    return scale * (
        h - jnp.mean(h, axis=-1, keepdims=True) - n * jnp.mean(h * n, axis=-1, keepdims=True)
    )


def row_mask(step, rows, limit):
    ids = lax.broadcasted_iota(jnp.int32, (rows, 1), 0) + step * rows
    return ids < limit


def cost(micros):
    return pl.CostEstimate(flops=0, bytes_accessed=int(micros * 3.7e6), transcendentals=0)


def whole(shape):
    zeros = (0,) * len(shape)
    return pl.BlockSpec(shape, lambda *_: zeros, pipeline_mode=pl.Buffered(1))


def project_kernel(at_ref, tok_ref, rel_ref, gain_ref, qkv_ref, w_ref):
    step = pl.program_id(0)

    @pl.when(step == 0)
    def _():
        x, y, core, z = at_ref[0], at_ref[1], at_ref[2], at_ref[3]
        for b in range(SHARDS):
            zb, yb, xb, cb = b // 8, (b // 4) % 2, (b // 2) % 2, b % 2
            j = (cb ^ core) * 16 + (yb ^ y) * 8 + (xb ^ x) * 4 + (zb ^ z)
            w_ref[b * SHARD : (b + 1) * SHARD, :] = rel_ref[j]

    values = jnp.where(row_mask(step, CH, TOK), tok_ref[...].astype(F32), 0.0)
    n, _ = normalise(values)
    normed = (n * gain_ref[...]).astype(BF16)
    for b in range(3):
        cols = dot_nn(normed, w_ref[b * D : (b + 1) * D, :])
        cols = cols.astype(BF16)
        qkv_ref[:, b * D : (b + 1) * D] = cols * HD ** (-0.5) if b == 0 else cols


def project(at, tokens, relative, gain):
    return pl.pallas_call(
        project_kernel,
        grid_spec=pltpu.PrefetchScalarGridSpec(
            num_scalar_prefetch=1,
            grid=(NCH,),
            in_specs=[
                pl.BlockSpec((CH, D), lambda i, a: (i, 0)),
                whole((SHARDS, SHARD, D)),
                whole((1, D)),
            ],
            out_specs=(
                pl.BlockSpec((CH, 3 * D), lambda i, a: (i, 0)),
                whole((4 * D, D)),
            ),
        ),
        out_shape=(
            jax.ShapeDtypeStruct((PAD, 3 * D), BF16),
            jax.ShapeDtypeStruct((4 * D, D), BF16),
        ),
        compiler_params=params(),
        cost_estimate=cost(10),
        name="project",
    )(at, tokens, relative, gain)


def window(image):
    start = image * SEQ
    base = pl.multiple_of((start // 16) * 16, 16)
    return base, start - base


def attend_kernel(first, per_step, qkv_ref, *refs):
    ctx_ref, probs_ref = refs[-2:]
    step = pl.program_id(0)

    @pl.when(step == 0)
    def _():
        ctx_ref[...] = refs[0][...] if first else jnp.zeros_like(ctx_ref)

    keys = lax.broadcasted_iota(jnp.int32, (1, KW), 1)
    rows = lax.broadcasted_iota(jnp.int32, (QW, 1), 0)
    lanes = lax.broadcasted_iota(jnp.int32, (1, 128), 1)
    for image in range(per_step):
        base, off = window(first + step * per_step + image)
        key_ok = jnp.logical_and(keys >= off, keys < off + SEQ)
        row_ok = jnp.logical_and(rows >= off, rows < off + SEQ)
        for pair in range(HEADS // 2):
            cols = pl.ds(pair * 128, 128)
            q = qkv_ref[pl.ds(base, QW), cols]
            k = qkv_ref[pl.ds(base, KW), pl.ds(D + pair * 128, 128)]
            v = qkv_ref[pl.ds(base, KW), pl.ds(2 * D + pair * 128, 128)]
            total = jnp.zeros((QW, 128), F32)
            for half in range(2):
                mine = jnp.logical_and(lanes >= half * HD, lanes < (half + 1) * HD)
                qh = jnp.where(mine, q, jnp.zeros_like(q))
                vh = jnp.where(mine, v, jnp.zeros_like(v))
                scores = jnp.where(key_ok, dot_nt(qh, k), NEG)
                raw = jnp.exp(scores - jnp.max(scores, axis=-1, keepdims=True))
                probs = (raw * (1.0 / jnp.sum(raw, axis=-1, keepdims=True))).astype(BF16)
                probs_ref[image, pair * 2 + half] = probs
                total = total + dot_nn(probs, vh)
            old = ctx_ref[pl.ds(base, QW), cols]
            ctx_ref[pl.ds(base, QW), cols] = jnp.where(row_ok, total.astype(BF16), old)


def attend(first, qkv, *old):
    per_step = 4
    return pl.pallas_call(
        functools.partial(attend_kernel, first, per_step),
        grid=(HALF // per_step,),
        out_shape=(
            jax.ShapeDtypeStruct((PAD, D), BF16),
            jax.ShapeDtypeStruct((HALF, HEADS, QW, KW), BF16),
        ),
        in_specs=[whole((PAD, 3 * D))] + [whole((PAD, D))] * len(old),
        out_specs=(
            pl.BlockSpec((PAD, D), lambda i: (0, 0), pipeline_mode=pl.Buffered(1)),
            pl.BlockSpec((per_step, HEADS, QW, KW), lambda i: (i, 0, 0, 0)),
        ),
        compiler_params=params(),
        cost_estimate=cost(15),
        name="attend",
    )(qkv, *old)


def dispatch_kernel(
    idx_ref, count_ref, ctx_ref, tok_ref, cot_ref, w_ref, gain_ref, rhi_ref, rlo_ref,
    res_ref, chance_ref, xg_ref, pg_ref, staged, table,
):
    step = pl.program_id(0)
    lanes = lax.broadcasted_iota(jnp.int32, (1, 128), 1)

    @pl.when(step < NCH)
    def _():
        residual = tok_ref[...].astype(F32) + dot_nn(ctx_ref[...], w_ref[...])
        res_ref[...] = residual
        n, _ = normalise(residual)
        normed = (n * gain_ref[...]).astype(BF16)
        logits = dot_nn(normed, rhi_ref[...]) + dot_nn(normed, rlo_ref[...])
        logits = jnp.where(lanes < E, logits, NEG)
        raw = jnp.exp(logits - jnp.max(logits, axis=-1, keepdims=True))
        chances = raw / jnp.sum(raw, axis=-1, keepdims=True)
        chance_ref[...] = chances
        wide = normed.astype(F32)
        cot = cot_ref[...].astype(F32)
        for j in range(3):
            part = slice(j * 128, (j + 1) * 128)
            staged[pl.ds(j, CH, stride=8), :] = wide[:, part]
            staged[pl.ds(3 + j, CH, stride=8), :] = cot[:, part]
        staged[pl.ds(6, CH, stride=8), :] = chances
        first = step * CH

        def place(i, carry):
            for u in range(16):
                c = i * 16 + u
                tile = staged[pl.ds(pl.multiple_of(c * 8, 8), 8), :]
                table[pl.ds(pl.multiple_of(idx_ref[first + c], 8), 8), :] = tile
                table[pl.ds(pl.multiple_of(idx_ref[PAD + first + c], 8), 8), :] = tile
            return carry

        lax.fori_loop(0, CH // 16, place, 0)

    @pl.when(step >= NCH)
    def _():
        expert = step - NCH
        used = lax.broadcasted_iota(jnp.int32, (ROWS, 1), 0) < count_ref[expert]
        at = pl.multiple_of(expert * (ROWS * 8), 8)
        for j in range(6):
            part = table[pl.ds(at + j, ROWS, stride=8), :]
            xg_ref[0, :, j * 128 : (j + 1) * 128] = jnp.where(used, part, 0.0).astype(BF16)
        pg_ref[0] = jnp.where(used, table[pl.ds(at + 6, ROWS, stride=8), :], 0.0)


def dispatch(idx, count, ctx, tokens, cotangent, weights, gain, rhi, rlo):
    chunk = lambda i, *_: (jnp.minimum(i, NCH - 1), 0)
    expert = lambda i, *_: (jnp.maximum(i - NCH, 0), 0, 0)
    return pl.pallas_call(
        dispatch_kernel,
        grid_spec=pltpu.PrefetchScalarGridSpec(
            num_scalar_prefetch=2,
            grid=(NCH + E,),
            in_specs=[
                pl.BlockSpec((CH, D), chunk),
                pl.BlockSpec((CH, D), chunk),
                pl.BlockSpec((CH, D), chunk),
                pl.BlockSpec((D, D), lambda i, *_: (3, 0), pipeline_mode=pl.Buffered(1)),
                whole((1, D)),
                whole((D, 128)),
                whole((D, 128)),
            ],
            out_specs=(
                pl.BlockSpec((CH, D), chunk),
                pl.BlockSpec((CH, 128), chunk),
                pl.BlockSpec((1, ROWS, 2 * D), expert),
                pl.BlockSpec((1, ROWS, 128), expert),
            ),
            scratch_shapes=[
                pltpu.VMEM((CH * 8, 128), F32),
                pltpu.VMEM(((ZERO_SLOT + 1) * 8, 128), F32),
            ],
        ),
        out_shape=(
            jax.ShapeDtypeStruct((TOK, D), F32),
            jax.ShapeDtypeStruct((TOK, 128), F32),
            jax.ShapeDtypeStruct((E, ROWS, 2 * D), BF16),
            jax.ShapeDtypeStruct((E, ROWS, 128), F32),
        ),
        compiler_params=params(),
        cost_estimate=cost(26),
        name="dispatch",
    )(idx, count, ctx, tokens, cotangent, weights, gain, rhi, rlo)


def gelu_parts(u):
    cdf = 0.5 + 0.5 * lax.erf(u * 0.5**0.5)
    return u * cdf, cdf + u * (jnp.exp(-0.5 * (u * u)) * 0.3989422804014327)


def expert_kernel(far, rel_y, at_ref, xg_ref, pg_ref, *refs):
    weights = refs[0:4]
    y_ref, gg_ref, keep0_ref, keep1_ref, send_ref = refs[4:9]
    win_s, wout_s, gwin_s, gwout_s, xt_s, gt_s, g_s, hid_s, gpre_s = refs[9:]
    x, y, core, z = at_ref[0], at_ref[1], at_ref[2], at_ref[3]
    expert = 2 * ((2 * far + pl.program_id(0)) ^ z) + (rel_y ^ y)
    place = [((r // 2) ^ x) * 2 + ((r % 2) ^ core) for r in range(4)]
    for r in range(4):
        rows = pl.ds(pl.multiple_of(place[r] * 96, 16), 96)
        for k in range(4):
            win_s[rows, k * D : (k + 1) * D] = weights[r][0, k * 96 : (k + 1) * 96, :]
        wout_s[pl.ds(pl.multiple_of(place[r] * D, 16), D), :] = weights[r][0, D : 2 * D, :]
    lanes = lax.broadcasted_iota(jnp.int32, (1, 128), 1)
    gate = jnp.sum(jnp.where(lanes == expert, pg_ref[0], 0.0), axis=-1, keepdims=True)
    g_s[...] = (gate * xg_ref[0, :, D:].astype(F32)).astype(BF16)
    xt_s[...] = xg_ref[0, :, :D].T
    gt_s[...] = g_s[...].T
    for c in range(FF // FCH):
        cols = slice(c * FCH, (c + 1) * FCH)
        pre = dot_nn(xg_ref[0, :, :D], win_s[:, cols])
        grad_hidden = dot_nt(g_s[...], wout_s[cols, :])
        value, slope = gelu_parts(pre)
        hid_s[:, cols] = value.astype(BF16)
        gpre_s[:, cols] = (grad_hidden * slope).astype(BF16)
    ret = dot_nn(hid_s[...], wout_s[...])
    back = dot_nt(gpre_s[...], win_s[...])
    gwout_s[...] = dot_nn(gt_s[...], hid_s[...]).astype(BF16)
    gwin_s[...] = dot_nn(xt_s[...], gpre_s[...]).astype(BF16)
    y_ref[0, :, :D] = (gate * ret).astype(BF16)
    y_ref[0, :, D:] = back.astype(BF16)
    grad_gate = jnp.sum(xg_ref[0, :, D:].astype(F32) * ret, axis=-1, keepdims=True)
    gg_ref[0] = jnp.where(lanes == expert, grad_gate, 0.0)
    for r in range(4):
        rows = pl.ds(pl.multiple_of(place[r] * 96, 16), 96)
        cols = pl.ds(pl.multiple_of(place[r] * D, 128), D)
        to = send_ref.at[r // 2, 0] if r % 2 else (keep0_ref, keep1_ref)[r // 2].at[0]
        for k in range(4):
            to[k * 96 : (k + 1) * 96, :] = gwin_s[rows, k * D : (k + 1) * D]
        to[D : 2 * D, :] = gwout_s[:, cols]


def experts(far, rel_y, at, xg, pg, weights):
    mine = lambda s, a: (2 * ((2 * far + s) ^ a[3]) + (rel_y ^ a[1]), 0, 0)
    step = lambda s, a: (s, 0, 0)
    block = pl.BlockSpec((1, 2 * D, D), step)
    grads = jax.ShapeDtypeStruct((2, 2 * D, D), BF16)
    return pl.pallas_call(
        functools.partial(expert_kernel, far, rel_y),
        grid_spec=pltpu.PrefetchScalarGridSpec(
            num_scalar_prefetch=1,
            grid=(2,),
            in_specs=[pl.BlockSpec((1, ROWS, 2 * D), mine), pl.BlockSpec((1, ROWS, 128), mine)]
            + [block] * 4,
            out_specs=[
                pl.BlockSpec((1, ROWS, 2 * D), step),
                pl.BlockSpec((1, ROWS, 128), step),
                block,
                block,
                pl.BlockSpec((2, 1, 2 * D, D), lambda s, a: (0, s, 0, 0)),
            ],
            scratch_shapes=[
                pltpu.VMEM((D, FF), BF16),
                pltpu.VMEM((FF, D), BF16),
                pltpu.VMEM((D, FF), BF16),
                pltpu.VMEM((D, FF), BF16),
                pltpu.VMEM((D, ROWS), BF16),
                pltpu.VMEM((D, ROWS), BF16),
                pltpu.VMEM((ROWS, D), BF16),
                pltpu.VMEM((ROWS, FF), BF16),
                pltpu.VMEM((ROWS, FF), BF16),
            ],
        ),
        out_shape=[
            jax.ShapeDtypeStruct((2, ROWS, 2 * D), BF16),
            jax.ShapeDtypeStruct((2, ROWS, 128), F32),
            grads,
            grads,
            jax.ShapeDtypeStruct((2, 2, 2 * D, D), BF16),
        ],
        compiler_params=params(),
        cost_estimate=cost(21),
        name="experts",
    )(at, xg, pg, *weights)


def combine_kernel(
    at_ref, idx_ref, y0_ref, y1_ref, y2_ref, y3_ref, gg0_ref, gg1_ref, gg2_ref, gg3_ref,
    res_ref, cot_ref, chance_ref, ctx_ref, w_ref, gain_ref, rhi_ref, rlo_ref,
    out_ref, gres_ref, gctx_ref, gwo_ref, ggain_ref, grouter_ref, table, summed,
):
    step = pl.program_id(0)

    @pl.when(step == 0)
    def _():
        table[pl.ds(ZERO_SLOT * 8, 8), :] = jnp.zeros((8, 128), F32)

    sources = ((y0_ref, gg0_ref), (y1_ref, gg1_ref), (y2_ref, gg2_ref), (y3_ref, gg3_ref))
    for call, (y_ref, gg_ref) in enumerate(sources):
        far, rel_y = ORDER[call]

        @pl.when(step // 2 == call)
        def _():
            expert = 2 * ((2 * far + step % 2) ^ at_ref[3]) + (rel_y ^ at_ref[1])
            to = pl.multiple_of(expert * (ROWS * 8), 8)
            for j in range(6):
                table[pl.ds(to + j, ROWS, stride=8), :] = y_ref[0, :, j * 128 : (j + 1) * 128].astype(F32)
            table[pl.ds(to + 6, ROWS, stride=8), :] = gg_ref[0]

    @pl.when(step >= E)
    def _():
        part = step - E
        first = part * CH

        def add(i, carry):
            for u in range(16):
                c = i * 16 + u
                one = pl.multiple_of(idx_ref[first + c], 8)
                two = pl.multiple_of(idx_ref[PAD + first + c], 8)
                summed[pl.ds(pl.multiple_of(c * 8, 8), 8), :] = table[pl.ds(one, 8), :] + table[pl.ds(two, 8), :]
            return carry

        lax.fori_loop(0, CH // 16, add, 0)
        ok = row_mask(part, CH, TOK)
        residual = jnp.where(ok, res_ref[...], 0.0)
        cot = jnp.where(ok, cot_ref[...].astype(F32), 0.0)
        chances = jnp.where(ok, chance_ref[...], 0.0)
        ctx = ctx_ref[...]
        ctx = jnp.where(ok, ctx, jnp.zeros_like(ctx))
        pieces = [summed[pl.ds(j, CH, stride=8), :] for j in range(7)]
        out_ref[...] = (residual + jnp.concatenate(pieces[0:3], axis=-1)).astype(BF16)
        grad_chances = pieces[6]
        grad_logits = chances * (
            grad_chances - jnp.sum(grad_chances * chances, axis=-1, keepdims=True)
        )
        high = grad_logits.astype(BF16)
        rest = (grad_logits - high.astype(F32)).astype(BF16)
        grad_normed = jnp.concatenate(pieces[3:6], axis=-1) + (
            dot_nt(high, rhi_ref[...]) + dot_nt(high, rlo_ref[...]) + dot_nt(rest, rhi_ref[...])
        )
        n, scale = normalise(residual)
        gain = gain_ref[...]
        normed = (n * gain).astype(BF16)
        grad_residual = cot + norm_pull(n, scale, grad_normed, gain)
        gres_ref[...] = grad_residual
        branch = jnp.where(ok, grad_residual, 0.0).astype(BF16)
        gctx_ref[...] = dot_nt(branch, w_ref[...]).astype(BF16)
        gwo = dot_tn(ctx, branch)
        ggain = jnp.sum(jnp.where(ok, grad_normed * n, 0.0), axis=0, keepdims=True)
        grouter = dot_tn(normed, high) + dot_tn(normed, rest)

        @pl.when(part == 0)
        def _():
            gwo_ref[...] = gwo
            ggain_ref[...] = ggain
            grouter_ref[...] = grouter

        @pl.when(part > 0)
        def _():
            gwo_ref[...] += gwo
            ggain_ref[...] += ggain
            grouter_ref[...] += grouter


def combine(at, idx, calls, res, cot, chances, ctx, weights, gain, rhi, rlo):
    chunk = lambda i, *_: (jnp.maximum(i - E, 0), 0)
    full = lambda shape: pl.BlockSpec(shape, lambda i, *_: (0,) * len(shape), pipeline_mode=pl.Buffered(1))
    turn = [lambda i, *_, c=c: (jnp.clip(i - 2 * c, 0, 1), 0, 0) for c in range(4)]
    fixed = lambda shape: pl.BlockSpec(shape, lambda i, *_: (0,) * len(shape))
    return pl.pallas_call(
        combine_kernel,
        grid_spec=pltpu.PrefetchScalarGridSpec(
            num_scalar_prefetch=2,
            grid=(E + NCH,),
            in_specs=[
                *[pl.BlockSpec((1, ROWS, 2 * D), turn[c]) for c in range(4)],
                *[pl.BlockSpec((1, ROWS, 128), turn[c]) for c in range(4)],
                pl.BlockSpec((CH, D), chunk),
                pl.BlockSpec((CH, D), chunk),
                pl.BlockSpec((CH, 128), chunk),
                pl.BlockSpec((CH, D), chunk),
                pl.BlockSpec((D, D), lambda i, *_: (3, 0), pipeline_mode=pl.Buffered(1)),
                full((1, D)),
                full((D, 128)),
                full((D, 128)),
            ],
            out_specs=(
                pl.BlockSpec((CH, D), chunk),
                pl.BlockSpec((CH, D), chunk),
                pl.BlockSpec((CH, D), chunk),
                fixed((D, D)),
                fixed((1, D)),
                fixed((D, 128)),
            ),
            scratch_shapes=[
                pltpu.VMEM(((ZERO_SLOT + 1) * 8, 128), F32),
                pltpu.VMEM((CH * 8, 128), F32),
            ],
        ),
        out_shape=(
            jax.ShapeDtypeStruct((TOK, D), BF16),
            jax.ShapeDtypeStruct((TOK, D), F32),
            jax.ShapeDtypeStruct((PAD, D), BF16),
            jax.ShapeDtypeStruct((D, D), F32),
            jax.ShapeDtypeStruct((1, D), F32),
            jax.ShapeDtypeStruct((D, 128), F32),
        ),
        compiler_params=params(),
        cost_estimate=cost(35),
        name="combine",
    )(at, idx, *[c[0] for c in calls], *[c[1] for c in calls], res, cot, chances, ctx, weights, gain, rhi, rlo)


def attend_back_kernel(qkv_ref, ctx_ref, gctx_ref, probs0_ref, probs1_ref, gqkv_ref):
    for half in range(2):

        @pl.when(pl.program_id(0) // HALF == half)
        def _():
            attend_back_image(qkv_ref, ctx_ref, gctx_ref, (probs0_ref, probs1_ref)[half], gqkv_ref)


def attend_back_image(qkv_ref, ctx_ref, gctx_ref, probs_ref, gqkv_ref):
    base, off = window(pl.program_id(0))
    rows = lax.broadcasted_iota(jnp.int32, (QW, 1), 0)
    row_ok = jnp.logical_and(rows >= off, rows < off + SEQ)
    wide = lax.broadcasted_iota(jnp.int32, (KW, 1), 0)
    wide_ok = jnp.logical_and(wide >= off, wide < off + SEQ)
    lanes = lax.broadcasted_iota(jnp.int32, (1, 128), 1)
    scale = HD ** (-0.5)
    for pair in range(HEADS // 2):
        cols = pl.ds(pair * 128, 128)
        cols_k = pl.ds(D + pair * 128, 128)
        cols_v = pl.ds(2 * D + pair * 128, 128)
        q = qkv_ref[pl.ds(base, QW), cols]
        k = qkv_ref[pl.ds(base, KW), cols_k]
        v = qkv_ref[pl.ds(base, KW), cols_v]
        grad = gctx_ref[pl.ds(base, QW), cols]
        grad = jnp.where(row_ok, grad, jnp.zeros_like(grad))
        ctx = ctx_ref[pl.ds(base, QW), cols]
        product = grad.astype(F32) * jnp.where(row_ok, ctx, jnp.zeros_like(ctx)).astype(F32)
        gq = jnp.zeros((QW, 128), F32)
        gk = jnp.zeros((KW, 128), F32)
        gv = jnp.zeros((KW, 128), F32)
        for half in range(2):
            mine = jnp.logical_and(lanes >= half * HD, lanes < (half + 1) * HD)
            grad_h = jnp.where(mine, grad, jnp.zeros_like(grad))
            q_h = jnp.where(mine, q, jnp.zeros_like(q))
            k_h = jnp.where(mine, k, jnp.zeros_like(k))
            mean = jnp.sum(jnp.where(mine, product, 0.0), axis=-1, keepdims=True)
            probs = probs_ref[0, pair * 2 + half]
            grad_probs = dot_nt(grad_h, v)
            grad_scores = (probs.astype(F32) * (grad_probs - mean)).astype(BF16)
            gv = gv + dot_tn(probs, grad_h)
            gq = gq + dot_nn(grad_scores, k_h)
            gk = gk + dot_tn(grad_scores, q_h)
        old = gqkv_ref[pl.ds(base, QW), cols]
        gqkv_ref[pl.ds(base, QW), cols] = jnp.where(row_ok, (gq * scale).astype(BF16), old)
        old = gqkv_ref[pl.ds(base, KW), cols_k]
        gqkv_ref[pl.ds(base, KW), cols_k] = jnp.where(wide_ok, gk.astype(BF16), old)
        old = gqkv_ref[pl.ds(base, KW), cols_v]
        gqkv_ref[pl.ds(base, KW), cols_v] = jnp.where(wide_ok, gv.astype(BF16), old)


def attend_back(qkv, ctx, gctx, probs0, probs1):
    return pl.pallas_call(
        attend_back_kernel,
        grid=(IMG,),
        out_shape=jax.ShapeDtypeStruct((PAD, 3 * D), BF16),
        in_specs=[
            whole((PAD, 3 * D)),
            whole((PAD, D)),
            whole((PAD, D)),
            pl.BlockSpec((1, HEADS, QW, KW), lambda i: (jnp.minimum(i, HALF - 1), 0, 0, 0)),
            pl.BlockSpec((1, HEADS, QW, KW), lambda i: (jnp.maximum(i - HALF, 0), 0, 0, 0)),
        ],
        out_specs=pl.BlockSpec((PAD, 3 * D), lambda i: (0, 0), pipeline_mode=pl.Buffered(1)),
        compiler_params=params(),
        cost_estimate=cost(27),
        name="attend_back",
    )(qkv, ctx, gctx, probs0, probs1)


def finish_kernel(
    at_ref, tok_ref, gqkv_ref, gres_ref, w_ref, gain_ref, gwo_ref, gtok_ref, rel_ref, ggain_ref, gw_s
):
    step = pl.program_id(0)
    ok = row_mask(step, CH, TOK)
    values = jnp.where(ok, tok_ref[...].astype(F32), 0.0)
    n, scale = normalise(values)
    gain = gain_ref[...]
    normed = (n * gain).astype(BF16)
    gqkv = gqkv_ref[...]
    gqkv = jnp.where(ok, gqkv, jnp.zeros_like(gqkv))
    grad = dot_nt(gqkv[:, 0:D], w_ref[0:D, :])
    for b in range(1, 3):
        grad = grad + dot_nt(gqkv[:, b * D : (b + 1) * D], w_ref[b * D : (b + 1) * D, :])
    gtok_ref[...] = (gres_ref[...] + norm_pull(n, scale, grad, gain)).astype(BF16)
    ggain = jnp.sum(grad * n, axis=0, keepdims=True)
    gw = dot_tn(normed, gqkv)

    @pl.when(step == 0)
    def _():
        gw_s[...] = gw
        ggain_ref[...] = ggain

    @pl.when(step > 0)
    def _():
        gw_s[...] += gw
        ggain_ref[...] += ggain

    @pl.when(step == NCH - 1)
    def _():
        x, y, core, z = at_ref[0], at_ref[1], at_ref[2], at_ref[3]
        for b in range(SHARDS):
            zb, yb, xb, cb = b // 8, (b // 4) % 2, (b // 2) % 2, b % 2
            j = (cb ^ core) * 16 + (yb ^ y) * 8 + (xb ^ x) * 4 + (zb ^ z)
            rows = slice((b % 8) * SHARD, (b % 8 + 1) * SHARD)
            part = gwo_ref[rows, :] if zb == 3 else gw_s[rows, zb * D : (zb + 1) * D]
            rel_ref[j] = part.astype(BF16)


def finish(at, tokens, gqkv, gres, weights, gain, gwo):
    chunk = lambda i, a: (i, 0)
    return pl.pallas_call(
        finish_kernel,
        grid_spec=pltpu.PrefetchScalarGridSpec(
            num_scalar_prefetch=1,
            grid=(NCH,),
            in_specs=[
                pl.BlockSpec((CH, D), chunk),
                pl.BlockSpec((CH, 3 * D), chunk),
                pl.BlockSpec((CH, D), chunk),
                whole((4 * D, D)),
                whole((1, D)),
                whole((D, D)),
            ],
            out_specs=(
                pl.BlockSpec((CH, D), chunk),
                whole((SHARDS, SHARD, D)),
                pl.BlockSpec((1, D), lambda i, a: (0, 0)),
            ),
            scratch_shapes=[pltpu.VMEM((D, 3 * D), F32)],
        ),
        out_shape=(
            jax.ShapeDtypeStruct((TOK, D), BF16),
            jax.ShapeDtypeStruct((SHARDS, SHARD, D), BF16),
            jax.ShapeDtypeStruct((1, D), F32),
        ),
        compiler_params=params(),
        cost_estimate=cost(15),
        name="finish",
    )(at, tokens, gqkv, gres, weights, gain, gwo)


def trade(value, bit, n):
    return lax.ppermute(value, "dp", [(i, i ^ bit) for i in range(n)])


def add_wide(*parts):
    total = parts[0].astype(F32)
    for part in parts[1:]:
        total = total + part.astype(F32)
    return total


def add_low(*parts):
    return add_wide(*parts).astype(BF16)


def pack_weights(w_in, w_out):
    rows = w_in.shape[0]
    return jnp.concatenate([w_in.reshape(rows, 4, D).swapaxes(0, 1).reshape(4 * rows, D), w_out])


def unpack_grads(value):
    rows = D // 4
    g_in = value[: 4 * rows].reshape(4, rows, D).swapaxes(0, 1).reshape(rows, FF)
    return g_in, value[4 * rows :].T


def join_calls(calls):
    blocks = {}
    for (far, rel_y), call in zip(ORDER, calls):
        for zr in range(2):
            for r in range(4):
                block = call[4][r // 2, zr] if r % 2 else call[2 + r // 2][zr]
                blocks[(2 * far + zr) * 8 + rel_y * 4 + r] = unpack_grads(block)
    return [jnp.concatenate([blocks[i][k] for i in range(SHARDS)]) for k in range(2)]


def prepare(routes, slots, gain_one, gain_two, router):
    idx = jnp.where(slots < CAP, routes * ROWS + slots, ZERO_SLOT).astype(jnp.int32).T
    idx = jnp.pad(idx, ((0, 0), (0, PAD - TOK)), constant_values=ZERO_SLOT).reshape(2 * PAD) * 8
    one_hot = routes[:, :, None] == jnp.arange(E, dtype=jnp.int32)[None, None, :]
    count = jnp.max(
        jnp.where(one_hot, jnp.minimum(slots + 1, CAP)[:, :, None], 0), axis=(0, 1)
    ).astype(jnp.int32)
    wide = jnp.pad(router, ((0, 0), (0, 128 - E)))
    rhi = wide.astype(BF16)
    rlo = (wide - rhi.astype(F32)).astype(BF16)
    return idx, count, gain_one.reshape(1, D), gain_two.reshape(1, D), rhi, rlo


def plain_layer(
    tokens, attn_weights, expert_in, expert_out, gain_one, gain_two, router, routes, slots,
    cotangent,
):
    at = jnp.zeros((4,), jnp.int32)
    full = lax.all_gather(attn_weights, "dp", axis=0, tiled=True).reshape(4, 2, 2, 2, SHARD, D)
    relative = full.transpose(3, 1, 2, 0, 4, 5).reshape(SHARDS, SHARD, D)
    all_in = lax.all_gather(expert_in, "dp", axis=0, tiled=True).reshape(SHARDS, D // 4, FF)
    all_out = lax.all_gather(expert_out, "dp", axis=0, tiled=True).reshape(SHARDS, D, D)
    packed = [pack_weights(all_in[i], all_out[i]) for i in range(SHARDS)]
    idx, count, one, two, rhi, rlo = prepare(routes, slots, gain_one, gain_two, router)
    qkv, weights = project(at, tokens, relative, one)
    ctx, probs0 = attend(0, qkv)
    ctx, probs1 = attend(HALF, qkv, ctx)
    res, chances, xg, pg = dispatch(idx, count, ctx, tokens, cotangent, weights, two, rhi, rlo)
    calls = []
    for far, rel_y in ORDER:
        blocks = [
            jnp.stack([packed[(2 * far + zr) * 8 + rel_y * 4 + r] for zr in range(2)])
            for r in range(4)
        ]
        calls.append(experts(far, rel_y, at, xg, pg, blocks))
    out, gres, gctx, gwo, ggain_two, grouter = combine(
        at, idx, calls, res, cotangent, chances, ctx, weights, two, rhi, rlo
    )
    gqkv = attend_back(qkv, ctx, gctx, probs0, probs1)
    gtok, grel, ggain_one = finish(at, tokens, gqkv, gres, weights, one, gwo)
    small = jnp.concatenate([ggain_one, ggain_two, grouter[:, :E].reshape(E, D)])
    gin, gout = join_calls(calls)
    gattn = grel.reshape(2, 2, 2, 4, SHARD, D).transpose(3, 1, 2, 0, 4, 5).reshape(4 * D, D)
    gin, gout, gattn = (
        lax.psum_scatter(g.astype(F32), "dp", scatter_dimension=0, tiled=True)
        for g in (gin, gout, gattn)
    )
    small = lax.psum(small, "dp")
    return out, gtok, gattn, gin, gout, small


def split_three(value):
    high = value.astype(BF16)
    rest = value - high.astype(F32)
    middle = rest.astype(BF16)
    low = (rest - middle.astype(F32)).astype(BF16)
    rows = jnp.concatenate([high, middle, low])
    return jnp.pad(rows, ((0, 32 - rows.shape[0]), (0, 0)))


def join_three(rows):
    wide = rows[:30].astype(F32)
    return (wide[:10] + wide[10:20]) + wide[20:30]


def beside(first, block, index):
    at = lax.broadcasted_iota(jnp.int32, (2, 1, 1), 0) == index
    return first.astype(F32) + jnp.where(at, block[None].astype(F32), 0.0)


def placed_layer(
    tokens, attn_weights, expert_in, expert_out, gain_one, gain_two, router, routes, slots,
    cotangent,
):
    n = SHARDS
    tie = lax.optimization_barrier
    me = lax.axis_index("dp")
    at = jnp.stack([(me >> 1) & 1, (me >> 2) & 1, me & 1, me >> 3]).astype(jnp.int32)
    ready = prepare(routes, slots, gain_one, gain_two, router)

    rel = jnp.stack([attn_weights] + [trade(attn_weights, 8 * j, n) for j in (1, 2, 3)])
    own = pack_weights(expert_in, expert_out)
    z_one = trade(own, 8, n)
    rel, own = tie((rel, own))
    rel = jnp.concatenate([rel] + [trade(rel, 2 * j, n) for j in (1, 2, 3)])
    z_two = trade(own, 16, n)
    rel = jnp.concatenate([rel, trade(rel, 1, n)])
    rel, at, ready, own, z_one = tie((rel, at, ready, own, z_one))
    idx, count, one, two, rhi, rlo = ready
    near = jnp.stack([own, z_one])
    near_x, near_y = trade(near, 2, n), trade(near, 4, n)
    rel, near = tie((rel, near))
    qkv, weights = project(at, tokens, rel, one)
    ctx, probs0 = attend(0, qkv)
    ctx, near_x, near_y, z_two = tie((ctx, near_x, near_y, z_two))
    z_three = trade(z_two, 8, n)
    near_c0, near_c1 = trade(near_x[0], 4, n), trade(near_y[1], 2, n)
    ctx, probs1 = attend(HALF, qkv, ctx)
    ctx, z_two, z_three, near_x, near_y, near_c0, near_c1 = tie(
        (ctx, z_two, z_three, near_x, near_y, near_c0, near_c1)
    )
    far = jnp.stack([z_two, z_three])
    far_x, far_y = trade(far, 2, n), trade(far, 4, n)
    near_, near_x_, near_y_ = (trade(v, 1, n) for v in (near, near_x, near_y))
    ctx, far = tie((ctx, far))
    res, chances, xg, pg = dispatch(idx, count, ctx, tokens, cotangent, weights, two, rhi, rlo)
    xg, far, far_x, far_y, near_, near_x_, near_y_ = tie(
        (xg, far, far_x, far_y, near_, near_x_, near_y_)
    )
    far_, far_x_, far_y_ = (trade(v, 1, n) for v in (far, far_x, far_y))
    far_c0, far_c1 = trade(far_x[0], 4, n), trade(far_y[1], 2, n)

    call0 = experts(1, 0, at, xg, pg, (far, far_, far_x, far_x_))
    (call0, far_c0, far_c1, far_y, far_y_) = tie((call0, far_c0, far_c1, far_y, far_y_))
    far_c, near_c = jnp.stack([far_c0, far_c1]), jnp.stack([near_c0, near_c1])
    far_c_, near_c_ = trade(far_c, 1, n), trade(near_c, 1, n)
    got0 = trade(call0[4], 1, n)
    call1 = experts(1, 1, at, xg, pg, (far_y, far_y_, far_c, far_c_))
    call1, near_c, near_c_, got0 = tie((call1, near_c, near_c_, got0))
    got1 = trade(call1[4], 1, n)
    call2 = experts(0, 1, at, xg, pg, (near_y, near_y_, near_c, near_c_))
    call2, got1 = tie((call2, got1))
    via_x = trade(add_low(call1[3][0], got1[1, 0]), 2, n)
    via_y = trade(add_low(call1[3][1], got1[1, 1]), 4, n)
    got2 = trade(call2[4], 1, n)
    call3 = experts(0, 0, at, xg, pg, (near, near_, near_x, near_x_))
    call3, got2, via_x, via_y = tie((call3, got2, via_x, via_y))
    far_rx = trade(beside(add_wide(call0[3], got0[1]), via_y, 1).astype(BF16), 2, n)
    far_ry = trade(beside(add_wide(call1[2], got1[0]), via_x, 0).astype(BF16), 4, n)
    via_x = trade(add_low(call2[3][0], got2[1, 0]), 2, n)
    via_y = trade(add_low(call2[3][1], got2[1, 1]), 4, n)
    got3 = trade(call3[4], 1, n)
    out, gres, gctx, gwo, ggain_two, grouter = combine(
        at, idx, (call0, call1, call2, call3), res, cotangent, chances, ctx, weights, two, rhi, rlo
    )
    gctx, far_rx, far_ry, via_x, via_y, got3 = tie((gctx, far_rx, far_ry, via_x, via_y, got3))
    far_three = trade(add_low(call0[2][1], got0[0, 1], far_rx[1], far_ry[1]), 8, n)
    near_rx = trade(beside(add_wide(call3[3], got3[1]), via_y, 1).astype(BF16), 2, n)
    near_ry = trade(beside(add_wide(call2[2], got2[0]), via_x, 0).astype(BF16), 4, n)
    gqkv = attend_back(qkv, ctx, gctx, probs0, probs1)
    gqkv, near_rx, near_ry, far_three = tie((gqkv, near_rx, near_ry, far_three))
    far_two = trade(add_low(call0[2][0], got0[0, 0], far_rx[0], far_ry[0], far_three), 16, n)
    near_one = trade(add_low(call3[2][1], got3[0, 1], near_rx[1], near_ry[1]), 8, n)
    gtok, grel, ggain_one = finish(at, tokens, gqkv, gres, weights, one, gwo)
    grel, ggain_one, near_one, far_two = tie((grel, ggain_one, near_one, far_two))
    small = split_three(
        jnp.concatenate([ggain_one, ggain_two, grouter[:, :E].reshape(E, D)])
    )
    got = trade(jnp.concatenate([grel[16:].reshape(16 * SHARD, D), small]), 1, n)
    both = add_low(grel[:16].reshape(16 * SHARD, D), got[: 16 * SHARD])
    small = split_three(join_three(small) + join_three(got[16 * SHARD :]))
    step = 4 * SHARD
    got = [
        trade(jnp.concatenate([both[j * step : (j + 1) * step], small]), 2 * j, n)
        for j in (1, 2, 3)
    ]
    total = add_wide(call3[2][0], got3[0, 0], near_rx[0], near_ry[0], near_one, far_two)
    gin, gout = unpack_grads(total)
    got, gin, gout = tie((got, gin, gout))
    mine = add_low(both[:step], *[g[:step] for g in got])
    parts = [join_three(g[step:]) for g in got]
    small = split_three((join_three(small) + parts[0]) + (parts[1] + parts[2]))
    got = [
        trade(jnp.concatenate([mine[j * SHARD : (j + 1) * SHARD], small]), 8 * j, n)
        for j in (1, 2, 3)
    ]
    gattn = add_wide(mine[:SHARD], *[g[:SHARD] for g in got])
    parts = [join_three(g[SHARD:]) for g in got]
    small = (join_three(small) + parts[0]) + (parts[1] + parts[2])
    return out, gtok, gattn, gin, gout, small


def on_device(devices, *args):
    layer = placed_layer if devices == SHARDS else plain_layer
    out, gtok, gattn, gin, gout, small = layer(*args)
    return out, gtok, gattn, gin, gout, small[0], small[1], small[2:].reshape(D, E)


def solution(mesh):
    split = P("dp", None)
    return jax.shard_map(
        functools.partial(on_device, mesh.shape["dp"]),
        mesh=mesh,
        in_specs=(split, split, split, split, P(), P(), P(), split, split, split),
        out_specs=(split, split, split, split, split, P(), P(), P()),
        check_vma=False,
    )
```

```python
import functools

import jax
import jax.numpy as jnp
from jax import lax
from jax.experimental import pallas as pl
from jax.experimental.pallas import tpu as pltpu
from jax.sharding import PartitionSpec as P

D = 384
HEADS = 6
FF = 1536
E = 8
SEQ = 197
IMG = 16
HD = 64
TOK = 3152
CAP = 788
ROWS = 800
CH = 800
NCH = 4
FOLD = 400
FOLD_STEPS = 8
PAD = CH * NCH
QW = 224
KW = 256
ZERO_SLOT = E * ROWS
EPSILON = 1e-06
NEG = -1e30
HALF = IMG // 2
FCH = 256
ORDER = ((0, 1), (0, 0), (1, 1), (1, 0))
F32 = jnp.float32
BF16 = jnp.bfloat16
MIB = 1 << 20
PROJECT_MIB, ATTEND_MIB, DISPATCH_MIB, EXPERTS_MIB = 16, 20, 44, 60
COMBINE_MIB, ATTEND_BACK_MIB, FINISH_MIB = 44, 16, 16
SHARDS = 32
WIDE = 2 * D + 128
SHARD = 4 * D // SHARDS


def dot_nn(a, b):
    return lax.dot_general(a, b, (((1,), (0,)), ((), ())), preferred_element_type=F32)


def dot_nt(a, b):
    return lax.dot_general(a, b, (((1,), (1,)), ((), ())), preferred_element_type=F32)


def dot_tn(a, b):
    return lax.dot_general(a, b, (((0,), (0,)), ((), ())), preferred_element_type=F32)


def params(limit=60):
    return pltpu.CompilerParams(
        dimension_semantics=("arbitrary",), vmem_limit_bytes=limit * MIB
    )


def normalise(values):
    centred = values - jnp.mean(values, axis=-1, keepdims=True)
    spread = jnp.mean(centred * centred, axis=-1, keepdims=True)
    scale = lax.rsqrt(spread + EPSILON)
    return centred * scale, scale


def norm_pull(n, scale, grad, gain):
    h = grad * gain
    return scale * (
        h - jnp.mean(h, axis=-1, keepdims=True) - n * jnp.mean(h * n, axis=-1, keepdims=True)
    )


def row_mask(step, rows, limit):
    ids = lax.broadcasted_iota(jnp.int32, (rows, 1), 0) + step * rows
    return ids < limit


def cost(micros):
    return pl.CostEstimate(flops=0, bytes_accessed=int(micros * 3.7e6), transcendentals=0)


def whole(shape):
    zeros = (0,) * len(shape)
    return pl.BlockSpec(shape, lambda *_: zeros, pipeline_mode=pl.Buffered(1))


def resident():
    return pl.BlockSpec(memory_space=pltpu.VMEM)


def project_kernel(at_ref, tok_ref, rel_ref, gain_ref, qkv_ref, w_ref):
    step = pl.program_id(0)

    @pl.when(step == 0)
    def _():
        x, y, core, z = at_ref[0], at_ref[1], at_ref[2], at_ref[3]
        for b in range(SHARDS):
            zb, yb, xb, cb = b // 8, (b // 4) % 2, (b // 2) % 2, b % 2
            j = (cb ^ core) * 16 + (yb ^ y) * 8 + (xb ^ x) * 4 + (zb ^ z)
            w_ref[b * SHARD : (b + 1) * SHARD, :] = rel_ref[j]

    values = jnp.where(row_mask(step, CH, TOK), tok_ref[...].astype(F32), 0.0)
    n, _ = normalise(values)
    normed = (n * gain_ref[...]).astype(BF16)
    rows = pl.ds(pl.multiple_of(step * CH, CH), CH)
    for b in range(3):
        cols = dot_nn(normed, w_ref[b * D : (b + 1) * D, :])
        cols = cols.astype(BF16)
        qkv_ref[rows, b * D : (b + 1) * D] = cols * HD ** (-0.5) if b == 0 else cols


def project(at, tokens, relative, gain):
    return pl.pallas_call(
        project_kernel,
        grid_spec=pltpu.PrefetchScalarGridSpec(
            num_scalar_prefetch=1,
            grid=(NCH,),
            in_specs=[
                pl.BlockSpec((CH, D), lambda i, a: (i, 0)),
                resident(),
                resident(),
            ],
            out_specs=(
                resident(),
                resident(),
            ),
        ),
        out_shape=(
            jax.ShapeDtypeStruct((PAD, 3 * D), BF16),
            jax.ShapeDtypeStruct((4 * D, D), BF16),
        ),
        compiler_params=params(PROJECT_MIB),
        cost_estimate=cost(10),
        name="project",
    )(at, tokens, relative, gain)


def window(image):
    start = image * SEQ
    base = pl.multiple_of((start // 16) * 16, 16)
    return base, start - base


def attend_kernel(first, per_step, qkv_ref, *refs):
    ctx_ref, probs_ref = refs[-2:]
    step = pl.program_id(0)

    @pl.when(step == 0)
    def _():
        ctx_ref[...] = refs[0][...] if first else jnp.zeros_like(ctx_ref)

    keys = lax.broadcasted_iota(jnp.int32, (1, KW), 1)
    rows = lax.broadcasted_iota(jnp.int32, (QW, 1), 0)
    lanes = lax.broadcasted_iota(jnp.int32, (1, 128), 1)
    for image in range(per_step):
        base, off = window(first + step * per_step + image)
        key_ok = jnp.logical_and(keys >= off, keys < off + SEQ)
        row_ok = jnp.logical_and(rows >= off, rows < off + SEQ)
        for pair in range(HEADS // 2):
            cols = pl.ds(pair * 128, 128)
            q = qkv_ref[pl.ds(base, QW), cols]
            k = qkv_ref[pl.ds(base, KW), pl.ds(D + pair * 128, 128)]
            v = qkv_ref[pl.ds(base, KW), pl.ds(2 * D + pair * 128, 128)]
            total = jnp.zeros((QW, 128), F32)
            for half in range(2):
                mine = jnp.logical_and(lanes >= half * HD, lanes < (half + 1) * HD)
                qh = jnp.where(mine, q, jnp.zeros_like(q))
                vh = jnp.where(mine, v, jnp.zeros_like(v))
                scores = jnp.where(key_ok, dot_nt(qh, k), NEG)
                raw = jnp.exp(scores - jnp.max(scores, axis=-1, keepdims=True))
                probs = (raw * (1.0 / jnp.sum(raw, axis=-1, keepdims=True))).astype(BF16)
                probs_ref[image, pair * 2 + half] = probs
                total = total + dot_nn(probs, vh)
            old = ctx_ref[pl.ds(base, QW), cols]
            ctx_ref[pl.ds(base, QW), cols] = jnp.where(row_ok, total.astype(BF16), old)


def attend(first, qkv, *old):
    per_step = 4
    return pl.pallas_call(
        functools.partial(attend_kernel, first, per_step),
        grid=(HALF // per_step,),
        out_shape=(
            jax.ShapeDtypeStruct((PAD, D), BF16),
            jax.ShapeDtypeStruct((HALF, HEADS, QW, KW), BF16),
        ),
        in_specs=[resident()] * (1 + len(old)),
        out_specs=(
            resident(),
            pl.BlockSpec((per_step, HEADS, QW, KW), lambda i: (i, 0, 0, 0)),
        ),
        compiler_params=params(ATTEND_MIB),
        cost_estimate=cost(15),
        name="attend",
    )(qkv, *old)


def dispatch_kernel(
    idx_ref, count_ref, ctx_ref, tok_ref, cot_ref, w_ref, gain_ref, rhi_ref, rlo_ref,
    res_ref, chance_ref, xg_ref, staged, table,
):
    step = pl.program_id(0)
    lanes = lax.broadcasted_iota(jnp.int32, (1, 128), 1)

    @pl.when(step < NCH)
    def _():
        rows = pl.ds(pl.multiple_of(step * CH, CH), CH)
        residual = tok_ref[...].astype(F32) + dot_nn(ctx_ref[rows, :], w_ref[3 * D : 4 * D, :])
        res_ref[...] = residual
        n, _ = normalise(residual)
        normed = (n * gain_ref[...]).astype(BF16)
        logits = dot_nn(normed, rhi_ref[...]) + dot_nn(normed, rlo_ref[...])
        logits = jnp.where(lanes < E, logits, NEG)
        raw = jnp.exp(logits - jnp.max(logits, axis=-1, keepdims=True))
        chances = raw / jnp.sum(raw, axis=-1, keepdims=True)
        chance_ref[...] = chances
        wide = normed.astype(F32)
        cot = cot_ref[...].astype(F32)
        for j in range(3):
            part = slice(j * 128, (j + 1) * 128)
            staged[pl.ds(j, CH, stride=8), :] = wide[:, part]
            staged[pl.ds(3 + j, CH, stride=8), :] = cot[:, part]
        high = chances.astype(BF16).astype(F32)
        staged[pl.ds(6, CH, stride=8), :] = high + pltpu.roll(chances - high, E, 1)
        first = step * CH

        def place(i, carry):
            for u in range(16):
                c = i * 16 + u
                tile = staged[pl.ds(pl.multiple_of(c * 8, 8), 8), :]
                table[pl.ds(pl.multiple_of(idx_ref[first + c], 8), 8), :] = tile
                table[pl.ds(pl.multiple_of(idx_ref[PAD + first + c], 8), 8), :] = tile
            return carry

        lax.fori_loop(0, CH // 16, place, 0)

    @pl.when(step >= NCH)
    def _():
        expert = step - NCH
        used = lax.broadcasted_iota(jnp.int32, (ROWS, 1), 0) < count_ref[expert]
        at = pl.multiple_of(expert * (ROWS * 8), 8)
        for j in range(7):
            part = table[pl.ds(at + j, ROWS, stride=8), :]
            xg_ref[0, :, j * 128 : (j + 1) * 128] = jnp.where(used, part, 0.0).astype(BF16)


def dispatch(idx, count, ctx, tokens, cotangent, weights, gain, rhi, rlo):
    chunk = lambda i, *_: (jnp.minimum(i, NCH - 1), 0)
    expert = lambda i, *_: (jnp.maximum(i - NCH, 0), 0, 0)
    return pl.pallas_call(
        dispatch_kernel,
        grid_spec=pltpu.PrefetchScalarGridSpec(
            num_scalar_prefetch=2,
            grid=(NCH + E,),
            in_specs=[
                resident(),
                pl.BlockSpec((CH, D), chunk),
                pl.BlockSpec((CH, D), chunk),
                *[resident()] * 4,
            ],
            out_specs=(
                pl.BlockSpec((CH, D), chunk),
                pl.BlockSpec((CH, 128), chunk),
                pl.BlockSpec((1, ROWS, WIDE), expert),
            ),
            scratch_shapes=[
                pltpu.VMEM((CH * 8, 128), F32),
                pltpu.VMEM(((ZERO_SLOT + 1) * 8, 128), F32),
            ],
        ),
        out_shape=(
            jax.ShapeDtypeStruct((TOK, D), F32),
            jax.ShapeDtypeStruct((TOK, 128), F32),
            jax.ShapeDtypeStruct((E, ROWS, WIDE), BF16),
        ),
        compiler_params=params(DISPATCH_MIB),
        cost_estimate=cost(26),
        name="dispatch",
    )(idx, count, ctx, tokens, cotangent, weights, gain, rhi, rlo)


def gelu_parts(u):
    cdf = 0.5 + 0.5 * lax.erf(u * 0.5**0.5)
    return u * cdf, cdf + u * (jnp.exp(-0.5 * (u * u)) * 0.3989422804014327)


def expert_kernel(far, rel_y, at_ref, xg_ref, *refs):
    weights = refs[0:4]
    y_ref, keep0_ref, keep1_ref, send_ref = refs[-13:-9]
    win_s, wout_s, gwin_s, gwout_s, xt_s, gt_s, g_s, hid_s, gpre_s = refs[-9:]
    x, y, core, z = at_ref[0], at_ref[1], at_ref[2], at_ref[3]
    expert = 2 * ((2 * far + pl.program_id(0)) ^ z) + (rel_y ^ y)
    place = [((r // 2) ^ x) * 2 + ((r % 2) ^ core) for r in range(4)]
    for r in range(4):
        rows = pl.ds(pl.multiple_of(place[r] * 96, 16), 96)
        for k in range(4):
            win_s[rows, k * D : (k + 1) * D] = weights[r][0, k * 96 : (k + 1) * 96, :]
        wout_s[pl.ds(pl.multiple_of(place[r] * D, 16), D), :] = weights[r][0, D : 2 * D, :]
    lanes = lax.broadcasted_iota(jnp.int32, (1, 128), 1)
    mine = jnp.logical_or(lanes == expert, lanes == expert + E)
    chances = xg_ref[0, :, 2 * D :].astype(F32)
    gate = jnp.sum(jnp.where(mine, chances, 0.0), axis=-1, keepdims=True)
    g_s[...] = (gate * xg_ref[0, :, D : 2 * D].astype(F32)).astype(BF16)
    xt_s[...] = xg_ref[0, :, :D].T
    gt_s[...] = g_s[...].T
    for c in range(FF // FCH):
        cols = slice(c * FCH, (c + 1) * FCH)
        pre = dot_nn(xg_ref[0, :, :D], win_s[:, cols])
        grad_hidden = dot_nt(g_s[...], wout_s[cols, :])
        value, slope = gelu_parts(pre)
        hid_s[:, cols] = value.astype(BF16)
        gpre_s[:, cols] = (grad_hidden * slope).astype(BF16)
    ret = dot_nn(hid_s[...], wout_s[...])
    back = dot_nt(gpre_s[...], win_s[...])
    gwout_s[...] = dot_nn(gt_s[...], hid_s[...]).astype(BF16)
    gwin_s[...] = dot_nn(xt_s[...], gpre_s[...]).astype(BF16)
    y_ref[0, :, :D] = (gate * ret).astype(BF16)
    y_ref[0, :, D : 2 * D] = back.astype(BF16)
    grad_gate = jnp.sum(xg_ref[0, :, D : 2 * D].astype(F32) * ret, axis=-1, keepdims=True)
    y_ref[0, :, 2 * D :] = jnp.where(lanes == expert, grad_gate, 0.0).astype(BF16)
    for r in range(4):
        rows = pl.ds(pl.multiple_of(place[r] * 96, 16), 96)
        cols = pl.ds(pl.multiple_of(place[r] * D, 128), D)
        to = send_ref.at[r // 2, 0] if r % 2 else (keep0_ref, keep1_ref)[r // 2].at[0]
        for k in range(4):
            to[k * 96 : (k + 1) * 96, :] = gwin_s[rows, k * D : (k + 1) * D]
        to[D : 2 * D, :] = gwout_s[:, cols]


def experts(turn, at, xg, weights, *y):
    far, rel_y = ORDER[turn]
    mine = lambda s, a: (2 * ((2 * far + s) ^ a[3]) + (rel_y ^ a[1]), 0, 0)
    block = pl.BlockSpec((1, 2 * D, D), lambda s, a: (s, 0, 0))
    grads = jax.ShapeDtypeStruct((2, 2 * D, D), BF16)
    return pl.pallas_call(
        functools.partial(expert_kernel, far, rel_y),
        grid_spec=pltpu.PrefetchScalarGridSpec(
            num_scalar_prefetch=1,
            grid=(2,),
            in_specs=[pl.BlockSpec((1, ROWS, WIDE), mine)]
            + [block] * 4
            + [pl.BlockSpec(memory_space=pl.ANY)] * len(y),
            out_specs=[
                pl.BlockSpec((1, ROWS, WIDE), lambda s, a: (2 * turn + s, 0, 0)),
                block,
                block,
                pl.BlockSpec((2, 1, 2 * D, D), lambda s, a: (0, s, 0, 0)),
            ],
            scratch_shapes=[
                pltpu.VMEM((D, FF), BF16),
                pltpu.VMEM((FF, D), BF16),
                pltpu.VMEM((D, FF), BF16),
                pltpu.VMEM((D, FF), BF16),
                pltpu.VMEM((D, ROWS), BF16),
                pltpu.VMEM((D, ROWS), BF16),
                pltpu.VMEM((ROWS, D), BF16),
                pltpu.VMEM((ROWS, FF), BF16),
                pltpu.VMEM((ROWS, FF), BF16),
            ],
        ),
        out_shape=[
            jax.ShapeDtypeStruct((E, ROWS, WIDE), BF16),
            grads,
            grads,
            jax.ShapeDtypeStruct((2, 2, 2 * D, D), BF16),
        ],
        input_output_aliases={6: 0} if y else {},
        compiler_params=params(EXPERTS_MIB),
        cost_estimate=cost(21),
        name="experts",
    )(at, xg, *weights, *y)


def combine_kernel(
    at_ref, idx_ref, y_ref, res_ref, cot_ref, chance_ref, ctx_ref, w_ref, gain_ref, rhi_ref, rlo_ref,
    out_ref, gres_ref, gctx_ref, gwo_ref, ggain_ref, grouter_ref, table, summed,
):
    step = pl.program_id(0)

    @pl.when(step == 0)
    def _():
        table[pl.ds(ZERO_SLOT * 8, 8), :] = jnp.zeros((8, 128), F32)

    for turn, (far, rel_y) in enumerate(ORDER):

        @pl.when(step // 2 == turn)
        def _():
            expert = 2 * ((2 * far + step % 2) ^ at_ref[3]) + (rel_y ^ at_ref[1])
            to = pl.multiple_of(expert * (ROWS * 8), 8)
            for j in range(7):
                part = y_ref[0, :, j * 128 : (j + 1) * 128]
                table[pl.ds(to + j, ROWS, stride=8), :] = part.astype(F32)

    @pl.when(step >= E)
    def _():
        part = step - E
        first = part * FOLD

        def add(i, carry):
            for u in range(16):
                c = i * 16 + u
                one = pl.multiple_of(idx_ref[first + c], 8)
                two = pl.multiple_of(idx_ref[PAD + first + c], 8)
                summed[pl.ds(pl.multiple_of(c * 8, 8), 8), :] = table[pl.ds(one, 8), :] + table[pl.ds(two, 8), :]
            return carry

        lax.fori_loop(0, FOLD // 16, add, 0)
        ok = row_mask(part, FOLD, TOK)
        residual = jnp.where(ok, res_ref[...], 0.0)
        cot = jnp.where(ok, cot_ref[...].astype(F32), 0.0)
        chances = jnp.where(ok, chance_ref[...], 0.0)
        rows = pl.ds(pl.multiple_of(part * FOLD, FOLD), FOLD)
        ctx = ctx_ref[rows, :]
        ctx = jnp.where(ok, ctx, jnp.zeros_like(ctx))
        pieces = [summed[pl.ds(j, FOLD, stride=8), :] for j in range(7)]
        out_ref[...] = (residual + jnp.concatenate(pieces[0:3], axis=-1)).astype(BF16)
        grad_chances = pieces[6]
        grad_logits = chances * (
            grad_chances - jnp.sum(grad_chances * chances, axis=-1, keepdims=True)
        )
        high = grad_logits.astype(BF16)
        rest = (grad_logits - high.astype(F32)).astype(BF16)
        grad_normed = jnp.concatenate(pieces[3:6], axis=-1) + (
            dot_nt(high, rhi_ref[...]) + dot_nt(high, rlo_ref[...]) + dot_nt(rest, rhi_ref[...])
        )
        n, scale = normalise(residual)
        gain = gain_ref[...]
        normed = (n * gain).astype(BF16)
        grad_residual = cot + norm_pull(n, scale, grad_normed, gain)
        gres_ref[...] = grad_residual
        branch = jnp.where(ok, grad_residual, 0.0).astype(BF16)
        gctx_ref[rows, :] = dot_nt(branch, w_ref[3 * D : 4 * D, :]).astype(BF16)
        gwo = dot_tn(ctx, branch)
        ggain = jnp.sum(jnp.where(ok, grad_normed * n, 0.0), axis=0, keepdims=True)
        grouter = dot_tn(normed, high) + dot_tn(normed, rest)

        @pl.when(part == 0)
        def _():
            gwo_ref[...] = gwo
            ggain_ref[...] = ggain
            grouter_ref[...] = grouter

        @pl.when(part > 0)
        def _():
            gwo_ref[...] += gwo
            ggain_ref[...] += ggain
            grouter_ref[...] += grouter


def combine(at, idx, y, res, cot, chances, ctx, weights, gain, rhi, rlo):
    chunk = lambda i, *_: (jnp.maximum(i - E, 0), 0)
    fixed = lambda shape: pl.BlockSpec(shape, lambda i, *_: (0,) * len(shape))
    return pl.pallas_call(
        combine_kernel,
        grid_spec=pltpu.PrefetchScalarGridSpec(
            num_scalar_prefetch=2,
            grid=(E + FOLD_STEPS,),
            in_specs=[
                pl.BlockSpec((1, ROWS, WIDE), lambda i, *_: (jnp.minimum(i, E - 1), 0, 0)),
                pl.BlockSpec((FOLD, D), chunk),
                pl.BlockSpec((FOLD, D), chunk),
                pl.BlockSpec((FOLD, 128), chunk),
                *[resident()] * 5,
            ],
            out_specs=(
                pl.BlockSpec((FOLD, D), chunk),
                pl.BlockSpec((FOLD, D), chunk),
                resident(),
                fixed((D, D)),
                fixed((1, D)),
                fixed((D, 128)),
            ),
            scratch_shapes=[
                pltpu.VMEM(((ZERO_SLOT + 1) * 8, 128), F32),
                pltpu.VMEM((FOLD * 8, 128), F32),
            ],
        ),
        out_shape=(
            jax.ShapeDtypeStruct((TOK, D), BF16),
            jax.ShapeDtypeStruct((TOK, D), F32),
            jax.ShapeDtypeStruct((PAD, D), BF16),
            jax.ShapeDtypeStruct((D, D), F32),
            jax.ShapeDtypeStruct((1, D), F32),
            jax.ShapeDtypeStruct((D, 128), F32),
        ),
        compiler_params=params(COMBINE_MIB),
        cost_estimate=cost(35),
        name="combine",
    )(at, idx, y, res, cot, chances, ctx, weights, gain, rhi, rlo)


def attend_back_kernel(per_step, qkv_ref, ctx_ref, gctx_ref, probs0_ref, probs1_ref, gqkv_ref):
    step = pl.program_id(0)
    for half in range(2):

        @pl.when(step // (HALF // per_step) == half)
        def _():
            for i in range(per_step):
                probs_ref = (probs0_ref, probs1_ref)[half].at[i]
                image = step * per_step + i
                attend_back_image(image, qkv_ref, ctx_ref, gctx_ref, probs_ref, gqkv_ref)


def attend_back_image(image, qkv_ref, ctx_ref, gctx_ref, probs_ref, gqkv_ref):
    base, off = window(image)
    rows = lax.broadcasted_iota(jnp.int32, (QW, 1), 0)
    row_ok = jnp.logical_and(rows >= off, rows < off + SEQ)
    wide = lax.broadcasted_iota(jnp.int32, (KW, 1), 0)
    wide_ok = jnp.logical_and(wide >= off, wide < off + SEQ)
    lanes = lax.broadcasted_iota(jnp.int32, (1, 128), 1)
    scale = HD ** (-0.5)
    for pair in range(HEADS // 2):
        cols = pl.ds(pair * 128, 128)
        cols_k = pl.ds(D + pair * 128, 128)
        cols_v = pl.ds(2 * D + pair * 128, 128)
        q = qkv_ref[pl.ds(base, QW), cols]
        k = qkv_ref[pl.ds(base, KW), cols_k]
        v = qkv_ref[pl.ds(base, KW), cols_v]
        grad = gctx_ref[pl.ds(base, QW), cols]
        grad = jnp.where(row_ok, grad, jnp.zeros_like(grad))
        ctx = ctx_ref[pl.ds(base, QW), cols]
        product = grad.astype(F32) * jnp.where(row_ok, ctx, jnp.zeros_like(ctx)).astype(F32)
        gq = jnp.zeros((QW, 128), F32)
        gk = jnp.zeros((KW, 128), F32)
        gv = jnp.zeros((KW, 128), F32)
        for half in range(2):
            mine = jnp.logical_and(lanes >= half * HD, lanes < (half + 1) * HD)
            grad_h = jnp.where(mine, grad, jnp.zeros_like(grad))
            q_h = jnp.where(mine, q, jnp.zeros_like(q))
            k_h = jnp.where(mine, k, jnp.zeros_like(k))
            mean = jnp.sum(jnp.where(mine, product, 0.0), axis=-1, keepdims=True)
            probs = probs_ref[pair * 2 + half]
            grad_probs = dot_nt(grad_h, v)
            grad_scores = (probs.astype(F32) * (grad_probs - mean)).astype(BF16)
            gv = gv + dot_tn(probs, grad_h)
            gq = gq + dot_nn(grad_scores, k_h)
            gk = gk + dot_tn(grad_scores, q_h)
        old = gqkv_ref[pl.ds(base, QW), cols]
        gqkv_ref[pl.ds(base, QW), cols] = jnp.where(row_ok, (gq * scale).astype(BF16), old)
        old = gqkv_ref[pl.ds(base, KW), cols_k]
        gqkv_ref[pl.ds(base, KW), cols_k] = jnp.where(wide_ok, gk.astype(BF16), old)
        old = gqkv_ref[pl.ds(base, KW), cols_v]
        gqkv_ref[pl.ds(base, KW), cols_v] = jnp.where(wide_ok, gv.astype(BF16), old)


def attend_back(qkv, ctx, gctx, probs0, probs1):
    per_step = 4
    steps = HALF // per_step
    block = (per_step, HEADS, QW, KW)
    return pl.pallas_call(
        functools.partial(attend_back_kernel, per_step),
        grid=(2 * steps,),
        out_shape=jax.ShapeDtypeStruct((PAD, 3 * D), BF16),
        in_specs=[
            *[resident()] * 3,
            pl.BlockSpec(block, lambda i: (jnp.minimum(i, steps - 1), 0, 0, 0)),
            pl.BlockSpec(block, lambda i: (jnp.maximum(i - steps, 0), 0, 0, 0)),
        ],
        out_specs=resident(),
        compiler_params=params(ATTEND_BACK_MIB),
        cost_estimate=cost(27),
        name="attend_back",
    )(qkv, ctx, gctx, probs0, probs1)


def finish_kernel(
    at_ref, tok_ref, gqkv_ref, gres_ref, w_ref, gain_ref, gwo_ref, gtok_ref, rel_ref, ggain_ref, gw_s
):
    step = pl.program_id(0)
    ok = row_mask(step, CH, TOK)
    values = jnp.where(ok, tok_ref[...].astype(F32), 0.0)
    n, scale = normalise(values)
    gain = gain_ref[...]
    normed = (n * gain).astype(BF16)
    gqkv = gqkv_ref[pl.ds(pl.multiple_of(step * CH, CH), CH), :]
    gqkv = jnp.where(ok, gqkv, jnp.zeros_like(gqkv))
    grad = dot_nt(gqkv[:, 0:D], w_ref[0:D, :])
    for b in range(1, 3):
        grad = grad + dot_nt(gqkv[:, b * D : (b + 1) * D], w_ref[b * D : (b + 1) * D, :])
    gtok_ref[...] = (gres_ref[...] + norm_pull(n, scale, grad, gain)).astype(BF16)
    ggain = jnp.sum(grad * n, axis=0, keepdims=True)
    gw = dot_tn(normed, gqkv)

    @pl.when(step == 0)
    def _():
        gw_s[...] = gw
        ggain_ref[...] = ggain

    @pl.when(step > 0)
    def _():
        gw_s[...] += gw
        ggain_ref[...] += ggain

    @pl.when(step == NCH - 1)
    def _():
        x, y, core, z = at_ref[0], at_ref[1], at_ref[2], at_ref[3]
        for b in range(SHARDS):
            zb, yb, xb, cb = b // 8, (b // 4) % 2, (b // 2) % 2, b % 2
            j = (cb ^ core) * 16 + (yb ^ y) * 8 + (xb ^ x) * 4 + (zb ^ z)
            rows = slice((b % 8) * SHARD, (b % 8 + 1) * SHARD)
            part = gwo_ref[rows, :] if zb == 3 else gw_s[rows, zb * D : (zb + 1) * D]
            rel_ref[j] = part.astype(BF16)


def finish(at, tokens, gqkv, gres, weights, gain, gwo):
    chunk = lambda i, a: (i, 0)
    return pl.pallas_call(
        finish_kernel,
        grid_spec=pltpu.PrefetchScalarGridSpec(
            num_scalar_prefetch=1,
            grid=(NCH,),
            in_specs=[
                pl.BlockSpec((CH, D), chunk),
                resident(),
                pl.BlockSpec((CH, D), chunk),
                *[resident()] * 3,
            ],
            out_specs=(
                pl.BlockSpec((CH, D), chunk),
                resident(),
                pl.BlockSpec((1, D), lambda i, a: (0, 0)),
            ),
            scratch_shapes=[pltpu.VMEM((D, 3 * D), F32)],
        ),
        out_shape=(
            jax.ShapeDtypeStruct((TOK, D), BF16),
            jax.ShapeDtypeStruct((SHARDS, SHARD, D), BF16),
            jax.ShapeDtypeStruct((1, D), F32),
        ),
        compiler_params=params(FINISH_MIB),
        cost_estimate=cost(15),
        name="finish",
    )(at, tokens, gqkv, gres, weights, gain, gwo)


def trade(value, bit, n):
    return lax.ppermute(value, "dp", [(i, i ^ bit) for i in range(n)])


def add_wide(*parts):
    total = parts[0].astype(F32)
    for part in parts[1:]:
        total = total + part.astype(F32)
    return total


def add_low(*parts):
    return add_wide(*parts).astype(BF16)


def pack_weights(w_in, w_out):
    rows = w_in.shape[0]
    return jnp.concatenate([w_in.reshape(rows, 4, D).swapaxes(0, 1).reshape(4 * rows, D), w_out])


def unpack_grads(value):
    rows = D // 4
    g_in = value[: 4 * rows].reshape(4, rows, D).swapaxes(0, 1).reshape(rows, FF)
    return g_in, value[4 * rows :].T


def join_calls(calls):
    blocks = {}
    for (far, rel_y), call in zip(ORDER, calls):
        for zr in range(2):
            for r in range(4):
                block = call[3][r // 2, zr] if r % 2 else call[1 + r // 2][zr]
                blocks[(2 * far + zr) * 8 + rel_y * 4 + r] = unpack_grads(block)
    return [jnp.concatenate([blocks[i][k] for i in range(SHARDS)]) for k in range(2)]


def prepare(routes, slots, gain_one, gain_two, router):
    idx = jnp.where(slots < CAP, routes * ROWS + slots, ZERO_SLOT).astype(jnp.int32).T
    idx = jnp.pad(idx, ((0, 0), (0, PAD - TOK)), constant_values=ZERO_SLOT).reshape(2 * PAD) * 8
    one_hot = routes[:, :, None] == jnp.arange(E, dtype=jnp.int32)[None, None, :]
    count = jnp.max(
        jnp.where(one_hot, jnp.minimum(slots + 1, CAP)[:, :, None], 0), axis=(0, 1)
    ).astype(jnp.int32)
    wide = jnp.pad(router, ((0, 0), (0, 128 - E)))
    rhi = wide.astype(BF16)
    rlo = (wide - rhi.astype(F32)).astype(BF16)
    return idx, count, gain_one.reshape(1, D), gain_two.reshape(1, D), rhi, rlo


def plain_layer(
    tokens, attn_weights, expert_in, expert_out, gain_one, gain_two, router, routes, slots,
    cotangent,
):
    at = jnp.zeros((4,), jnp.int32)
    full = lax.all_gather(attn_weights, "dp", axis=0, tiled=True).reshape(4, 2, 2, 2, SHARD, D)
    relative = full.transpose(3, 1, 2, 0, 4, 5).reshape(SHARDS, SHARD, D)
    all_in = lax.all_gather(expert_in, "dp", axis=0, tiled=True).reshape(SHARDS, D // 4, FF)
    all_out = lax.all_gather(expert_out, "dp", axis=0, tiled=True).reshape(SHARDS, D, D)
    packed = [pack_weights(all_in[i], all_out[i]) for i in range(SHARDS)]
    idx, count, one, two, rhi, rlo = prepare(routes, slots, gain_one, gain_two, router)
    qkv, weights = project(at, tokens, relative, one)
    ctx, probs0 = attend(0, qkv)
    ctx, probs1 = attend(HALF, qkv, ctx)
    res, chances, xg = dispatch(idx, count, ctx, tokens, cotangent, weights, two, rhi, rlo)
    calls = []
    y = ()
    for turn, (far, rel_y) in enumerate(ORDER):
        blocks = [
            jnp.stack([packed[(2 * far + zr) * 8 + rel_y * 4 + r] for zr in range(2)])
            for r in range(4)
        ]
        calls.append(experts(turn, at, xg, blocks, *y))
        y = calls[-1][:1]
    out, gres, gctx, gwo, ggain_two, grouter = combine(
        at, idx, *y, res, cotangent, chances, ctx, weights, two, rhi, rlo
    )
    gqkv = attend_back(qkv, ctx, gctx, probs0, probs1)
    gtok, grel, ggain_one = finish(at, tokens, gqkv, gres, weights, one, gwo)
    small = jnp.concatenate([ggain_one, ggain_two, grouter[:, :E].reshape(E, D)])
    gin, gout = join_calls(calls)
    gattn = grel.reshape(2, 2, 2, 4, SHARD, D).transpose(3, 1, 2, 0, 4, 5).reshape(4 * D, D)
    gin, gout, gattn = (
        lax.psum_scatter(g.astype(F32), "dp", scatter_dimension=0, tiled=True)
        for g in (gin, gout, gattn)
    )
    small = lax.psum(small, "dp")
    return out, gtok, gattn, gin, gout, small


def split_three(value):
    high = value.astype(BF16)
    rest = value - high.astype(F32)
    middle = rest.astype(BF16)
    low = (rest - middle.astype(F32)).astype(BF16)
    rows = jnp.concatenate([high, middle, low])
    return jnp.pad(rows, ((0, 32 - rows.shape[0]), (0, 0)))


def join_three(rows):
    wide = rows[:30].astype(F32)
    return (wide[:10] + wide[10:20]) + wide[20:30]


def beside(block, index):
    return jnp.pad(block[None], ((index, 1 - index), (0, 0), (0, 0)))


def placed_layer(
    tokens, attn_weights, expert_in, expert_out, gain_one, gain_two, router, routes, slots,
    cotangent,
):
    n = SHARDS
    tie = lax.optimization_barrier
    me = lax.axis_index("dp")
    at = jnp.stack([(me >> 1) & 1, (me >> 2) & 1, me & 1, me >> 3]).astype(jnp.int32)
    ready = prepare(routes, slots, gain_one, gain_two, router)

    rel = jnp.stack([attn_weights] + [trade(attn_weights, 8 * j, n) for j in (1, 2, 3)])
    own = pack_weights(expert_in, expert_out)
    z_one = trade(own, 8, n)
    rel, own = tie((rel, own))
    rel = jnp.concatenate([rel] + [trade(rel, 2 * j, n) for j in (1, 2, 3)])
    rel = jnp.concatenate([rel, trade(rel, 1, n)])
    rel, at, ready, own, z_one = tie((rel, at, ready, own, z_one))
    idx, count, one, two, rhi, rlo = ready
    near = jnp.stack([own, z_one])
    near_x, near_y = trade(near, 2, n), trade(near, 4, n)
    rel, near = tie((rel, near))
    qkv, weights = project(at, tokens, rel, one)
    z_two = trade(own, 16, n)
    ctx, probs0 = attend(0, qkv)
    ctx, probs1 = attend(HALF, qkv, ctx)
    ctx, z_two, near_x, near_y = tie((ctx, z_two, near_x, near_y))
    near_c0, near_c1 = trade(near_x[0], 4, n), trade(near_y[1], 2, n)
    z_three = trade(z_two, 8, n)
    near_, near_x_, near_y_ = (trade(v, 1, n) for v in (near, near_x, near_y))
    res, chances, xg = dispatch(idx, count, ctx, tokens, cotangent, weights, two, rhi, rlo)
    xg, z_two, z_three, near_c0, near_c1, near_, near_x_, near_y_ = tie(
        (xg, z_two, z_three, near_c0, near_c1, near_, near_x_, near_y_)
    )
    near_c = jnp.stack([near_c0, near_c1])
    near_c_ = trade(near_c, 1, n)
    far = jnp.stack([z_two, z_three])
    far_x, far_y = trade(far, 2, n), trade(far, 4, n)
    far_ = trade(far, 1, n)

    call0 = experts(0, at, xg, (near_y, near_y_, near_c, near_c_))
    call0, far, far_, far_x, far_y = tie((call0, far, far_, far_x, far_y))
    far_c0, far_c1 = trade(far_x[0], 4, n), trade(far_y[1], 2, n)
    got0 = trade(call0[3], 1, n)
    far_x_, far_y_ = trade(far_x, 1, n), trade(far_y, 1, n)
    call1 = experts(1, at, xg, (near, near_, near_x, near_x_), call0[0])
    call1, got0, far_c0, far_c1, far_x_, far_y_ = tie(
        (call1, got0, far_c0, far_c1, far_x_, far_y_)
    )
    far_c = jnp.stack([far_c0, far_c1])
    far_c_ = trade(far_c, 1, n)
    via_x = trade(add_low(call0[2][0], got0[1, 0]), 2, n)
    via_y = trade(add_low(call0[2][1], got0[1, 1]), 4, n)
    got1 = trade(call1[3], 1, n)
    call2 = experts(2, at, xg, (far_y, far_y_, far_c, far_c_), call1[0])
    call2, got1, via_x, via_y = tie((call2, got1, via_x, via_y))
    near_gx = trade(add_low(call1[2], got1[1], beside(via_y, 1)), 2, n)
    near_gy = trade(add_low(call0[1], got0[0], beside(via_x, 0)), 4, n)
    got2 = trade(call2[3], 1, n)
    call3 = experts(3, at, xg, (far, far_, far_x, far_x_), call2[0])
    call3, got2, near_gx, near_gy = tie((call3, got2, near_gx, near_gy))
    via_x = trade(add_low(call2[2][0], got2[1, 0]), 2, n)
    via_y = trade(add_low(call2[2][1], got2[1, 1]), 4, n)
    got3 = trade(call3[3], 1, n)
    near_one = trade(add_low(call1[1][1], got1[0, 1], near_gx[1], near_gy[1]), 8, n)
    out, gres, gctx, gwo, ggain_two, grouter = combine(
        at, idx, call3[0], res, cotangent, chances, ctx, weights, two, rhi, rlo
    )
    gctx, via_x, via_y, got3, near_one = tie((gctx, via_x, via_y, got3, near_one))
    far_gx = trade(add_low(call3[2], got3[1], beside(via_y, 1)), 2, n)
    far_gy = trade(add_low(call2[1], got2[0], beside(via_x, 0)), 4, n)
    gqkv = attend_back(qkv, ctx, gctx, probs0, probs1)
    gqkv, far_gx, far_gy = tie((gqkv, far_gx, far_gy))
    far_three = trade(add_low(call3[1][1], got3[0, 1], far_gx[1], far_gy[1]), 8, n)
    gtok, grel, ggain_one = finish(at, tokens, gqkv, gres, weights, one, gwo)
    grel, ggain_one, far_three = tie((grel, ggain_one, far_three))
    far_two = add_low(call3[1][0], got3[0, 0], far_gx[0], far_gy[0], far_three)
    two_in, two_out = trade(far_two[:D], 16, n), trade(far_two[D:], 16, n)
    small = split_three(
        jnp.concatenate([ggain_one, ggain_two, grouter[:, :E].reshape(E, D)])
    )
    got = trade(jnp.concatenate([grel[16:].reshape(16 * SHARD, D), small]), 1, n)
    both = add_low(grel[:16].reshape(16 * SHARD, D), got[: 16 * SHARD])
    small = split_three(join_three(small) + join_three(got[16 * SHARD :]))
    step = 4 * SHARD
    got = [
        trade(jnp.concatenate([both[j * step : (j + 1) * step], small]), 2 * j, n)
        for j in (1, 2, 3)
    ]
    got, two_in = tie((got, two_in))
    mine = add_low(both[:step], *[g[:step] for g in got])
    parts = [join_three(g[step:]) for g in got]
    small = split_three((join_three(small) + parts[0]) + (parts[1] + parts[2]))
    got = [
        trade(jnp.concatenate([mine[j * SHARD : (j + 1) * SHARD], small]), 8 * j, n)
        for j in (1, 2, 3)
    ]
    parts_in = [v[:D] for v in (call1[1][0], got1[0, 0], near_gx[0], near_gy[0], near_one)]
    gin = add_wide(*parts_in, two_in).reshape(4, D // 4, D).swapaxes(0, 1).reshape(D // 4, FF)
    got, two_out, gin = tie((got, two_out, gin))
    gattn = add_wide(mine[:SHARD], *[g[:SHARD] for g in got])
    parts_out = [v[D:] for v in (call1[1][0], got1[0, 0], near_gx[0], near_gy[0], near_one)]
    gout = add_wide(*parts_out, two_out).T
    parts = [join_three(g[SHARD:]) for g in got]
    small = (join_three(small) + parts[0]) + (parts[1] + parts[2])
    return out, gtok, gattn, gin, gout, small


def on_device(devices, *args):
    layer = placed_layer if devices == SHARDS else plain_layer
    out, gtok, gattn, gin, gout, small = layer(*args)
    return out, gtok, gattn, gin, gout, small[0], small[1], small[2:].reshape(D, E)


def solution(mesh):
    split = P("dp", None)
    return jax.shard_map(
        functools.partial(on_device, mesh.shape["dp"]),
        mesh=mesh,
        in_specs=(split, split, split, split, P(), P(), P(), split, split, split),
        out_specs=(split, split, split, split, split, P(), P(), P()),
        check_vma=False,
    )
```
